128 devices in a mesh: section: 4 (over x_hi, core), dom: 32 (over z, y, x_lo).
Axes of the slice: x: 4 (x_hi: 2, x_lo: 2; x = x_hi * 2 + x_lo), y: 4, z: 4, core: 2. Of those that a mesh axis runs over, the one named last changes fastest.
Arguments:
- voltages: bfloat16 [512, 64, 2048], P('dom'), may hold values from -6 to 6
- station_map: int32 [512], replicated, may hold values from 0 to 511, each once
- beam_table: int32 [128, 512], replicated, may hold values from 0 to 63
- weight_table: bfloat16 [2, 64, 1024], P(None, None, 'dom'), may hold values from -0.3125 to 0.3125
- dm_trial: int32 [128], replicated, may hold values from 0 to 31
Outputs:
- power: float32 [128, 64, 1024], P(('section', 'dom'))
The draws below stay inside these ranges and needn't reach their ends.
Inputs may be any that keep to these rules, and one draw needn't show every extreme that they name: `station_map`: each of the 512 stations appears once.
All inputs are finite; a program needn't handle non-finite values.
Results may differ from the reference program's by a relative error of at most 0.0042.
Values may be sent and summed in bfloat16 or wider, within the bound.
No kernel may reach another device: no remote copies, remote signals or barrier semaphores. Data moves between devices by JAX's collectives and lax.ppermute only.
A program may use at most 128 MiB of HBM per device.

```python
import math
import jax
import jax.numpy as jnp
from jax import lax

NSTAT = 512
NFFT = 2048
CH = 1024
BEAMS = 128
NTAB = 64
FRAMES = 64
NDM = 32


def place_ends(values, stream_key, smallest, largest):
    longest = values.shape.index(max(values.shape))
    spots = []
    for shift in (0, 1):
        where = [jax.random.randint(jax.random.fold_in(stream_key, axis), (), 0, length) for axis, length in enumerate(values.shape)]
        where[longest] = (where[longest] + shift) % values.shape[longest]
        spots.append(tuple(where))
    return values.at[spots[0]].set(smallest).at[spots[1]].set(largest)


def level_of(stream_key, dims, pieces, least, largest):
    factor_of, own = 1.0, jax.random.fold_in(stream_key, 6)
    for axis_at, blocks in pieces:
        heights = jnp.exp(jax.random.uniform(jax.random.fold_in(own, axis_at), (blocks,), jnp.float32, least / len(pieces), largest / len(pieces)))
        factor_of = factor_of * jnp.repeat(heights, dims[axis_at] // blocks).reshape([-1 if axis == axis_at else 1 for axis in range(len(dims))])
    return factor_of


def normal_values(rng, shape, scale, reach, cuts=(), kind=jnp.bfloat16):
    entries = scale * jax.random.normal(rng, shape, jnp.float32)
    if cuts:
        entries = entries * level_of(rng, shape, cuts, -0.22, 0.18)
    return jnp.clip(entries, -reach, reach).astype(kind)


def setup_inputs(seed: int = 0) -> dict:
    key_list = jax.random.split(jax.random.key(seed), 6)
    return {
        "voltages": normal_values(key_list[0], (NSTAT, FRAMES, NFFT), 1.0, 6.0, ((0, 32),)),
        "station_map": jax.random.permutation(key_list[1], NSTAT).astype(jnp.int32),
        "beam_table": place_ends(jax.random.randint(key_list[2], (BEAMS, NSTAT), 0, NTAB), jax.random.fold_in(key_list[2], 1), 0, NTAB - 1).astype(jnp.int32),
        "weight_table": normal_values(key_list[3], (2, NTAB, CH), (3 * NSTAT // 4) ** -0.5, 0.3125, ((2, 32),)),
        "dm_trial": place_ends(jax.random.randint(key_list[4], (BEAMS,), 0, NDM), jax.random.fold_in(key_list[4], 1), 0, NDM - 1).astype(jnp.int32),
    }


def dft_table():
    sample_index = jnp.arange(NFFT, dtype=jnp.int32)
    window = 0.5 - 0.5 * jnp.cos(sample_index.astype(jnp.float32) * (2.0 * math.pi / NFFT))
    column = jnp.arange(NFFT, dtype=jnp.int32)
    bin_index = column % CH
    product = sample_index[:, None] * bin_index[None, :] % NFFT
    angle = product.astype(jnp.float32) * (2.0 * math.pi / NFFT)
    values = jnp.where(column[None, :] < CH, jnp.cos(angle), -jnp.sin(angle))
    return (values * (window[:, None] / math.sqrt(NFFT))).astype(jnp.bfloat16)

def reference(voltages, station_map, beam_table, weight_table, dm_trial):
    table = dft_table()
    flat = voltages.reshape(NSTAT * FRAMES, NFFT)
    spectra = jnp.dot(flat, table, preferred_element_type=jnp.float32).reshape(NSTAT, FRAMES, NFFT)
    chan_re = spectra[:, :, :CH].astype(jnp.bfloat16)
    chan_im = spectra[:, :, CH:].astype(jnp.bfloat16)
    ordered = beam_table[:, station_map]
    block_size = min(64, CH)

    def form(block_index):
        start = (block_index * block_size).astype(jnp.int32)
        table_re = lax.dynamic_slice_in_dim(weight_table[0], start, block_size, 1)
        table_im = lax.dynamic_slice_in_dim(weight_table[1], start, block_size, 1)
        w_re = table_re[ordered].astype(jnp.float32)
        w_im = table_im[ordered].astype(jnp.float32)
        x_re = lax.dynamic_slice_in_dim(chan_re, start, block_size, 2).astype(jnp.float32)
        x_im = lax.dynamic_slice_in_dim(chan_im, start, block_size, 2).astype(jnp.float32)
        beam_re = jnp.einsum('bsc,sfc->bfc', w_re, x_re) - jnp.einsum('bsc,sfc->bfc', w_im, x_im)
        beam_im = jnp.einsum('bsc,sfc->bfc', w_re, x_im) + jnp.einsum('bsc,sfc->bfc', w_im, x_re)
        return (beam_re, beam_im)
    blocks_re, blocks_im = lax.map(form, jnp.arange(CH // block_size, dtype=jnp.int32))
    beams_re = jnp.transpose(blocks_re, (1, 2, 0, 3)).reshape(BEAMS, FRAMES, CH)
    beams_im = jnp.transpose(blocks_im, (1, 2, 0, 3)).reshape(BEAMS, FRAMES, CH)
    spectrum = jnp.fft.fft(beams_re + 1j * beams_im, axis=1)
    bins = jnp.arange(FRAMES, dtype=jnp.int32)
    kappa = jnp.where(bins < FRAMES // 2, bins, bins - FRAMES).astype(jnp.float32)
    freq = 1.0 + jnp.arange(CH, dtype=jnp.float32) / CH
    spread = 1.0 / (freq * freq * freq)
    measure = (dm_trial + 1).astype(jnp.float32) / NDM
    coeff = math.pi * measure[:, None] * spread[None, :]
    phase = coeff[:, None, :] * (kappa * kappa / FRAMES)[None, :, None]
    rotated = spectrum * (jnp.cos(phase) + 1j * jnp.sin(phase))
    series = jnp.fft.ifft(rotated, axis=1)
    power = jnp.real(series) * jnp.real(series) + jnp.imag(series) * jnp.imag(series)
    return power.astype(jnp.float32)
```

```python
import math

import jax
import jax.numpy as jnp
import ml_dtypes
import numpy as np
from jax import lax
from jax.experimental import pallas as pl
from jax.experimental.pallas import tpu as pltpu
from jax.sharding import PartitionSpec as P

NSTAT = 512
NFFT = 2048
CH = 1024
BEAMS = 128
NTAB = 64
FRAMES = 64
NDM = 32
SECTIONS = 4
DOMS = 32
STATIONS = NSTAT // DOMS
MINE = CH // (SECTIONS * DOMS)
LANES = 128
COLS = 2 * CH // SECTIONS
STEPS = 4
NT = (((1,), (1,)), ((), ()))
F32 = jnp.float32
BF16 = jnp.bfloat16


def dft_table():
    sample = np.arange(NFFT)
    window = 0.5 - 0.5 * np.cos(sample.astype(np.float32) * np.float32(2.0 * math.pi / NFFT))
    scale = (window / np.float32(math.sqrt(NFFT))).astype(np.float32)
    angle = (np.arange(CH)[:, None] * sample[None, :] % NFFT).astype(np.float32) * np.float32(
        2.0 * math.pi / NFFT
    )
    parts = np.stack((np.cos(angle) * scale, -np.sin(angle) * scale))
    parts = parts.reshape(2, DOMS, SECTIONS, MINE, NFFT).transpose(2, 1, 0, 3, 4)
    return parts.reshape(SECTIONS, COLS, NFFT).astype(ml_dtypes.bfloat16)


def frame_tables():
    index = np.arange(FRAMES)
    angle = (index[:, None] * index[None, :] % FRAMES) * (2.0 * math.pi / FRAMES)
    cosine, sine = np.cos(angle), np.sin(angle)
    forward = np.block([[cosine, -sine], [sine, cosine]])
    inverse = np.block([[cosine, sine], [-sine, cosine]]) / FRAMES
    tables = []
    for table in (forward, inverse):
        high = table.astype(ml_dtypes.bfloat16)
        tables += [high, (table - high.astype(np.float64)).astype(ml_dtypes.bfloat16)]
    return np.stack(tables)


def channelise_kernel(table_hbm, volts_hbm, out_ref, table, volts, turned, table_sem, volts_sem):
    section = lax.axis_index("section")
    share = STATIONS * FRAMES // STEPS
    get_table = pltpu.make_async_copy(table_hbm.at[section], table, table_sem)
    get_volts = [
        pltpu.make_async_copy(
            volts_hbm.at[pl.ds(n * share, share)], volts.at[n], volts_sem.at[n]
        )
        for n in range(STEPS)
    ]
    get_volts[0].start()
    get_table.start()
    for n in range(1, STEPS):
        get_volts[n].start()
    get_table.wait()
    low = lax.broadcasted_iota(jnp.int32, (8, LANES), 1) < FRAMES
    for n in range(STEPS):
        get_volts[n].wait()
        spectrum = lax.dot_general(table[...], volts[n], NT, preferred_element_type=F32)
        for d in range(DOMS):
            for t in range(share // LANES):
                real = spectrum[16 * d : 16 * d + 8, LANES * t : LANES * (t + 1)]
                imag = spectrum[16 * d + 8 : 16 * d + 16, LANES * t : LANES * (t + 1)]
                station = (n * share + t * LANES) // FRAMES
                base = d * MINE * STATIONS + station
                turned[pl.ds(base, 8, stride=STATIONS), :] = jnp.where(
                    low, real, pltpu.roll(imag, FRAMES, 1)
                )
                turned[pl.ds(base + 1, 8, stride=STATIONS), :] = jnp.where(
                    low, pltpu.roll(real, FRAMES, 1), imag
                )
    for d in range(DOMS):
        out_ref[d] = turned[pl.ds(d * LANES, LANES), :].astype(BF16)


def channelise(table, volts):
    return pl.pallas_call(
        channelise_kernel,
        name="channelise",
        out_shape=jax.ShapeDtypeStruct((DOMS, MINE * STATIONS, LANES), BF16),
        in_specs=[pl.BlockSpec(memory_space=pl.ANY)] * 2,
        out_specs=pl.BlockSpec(memory_space=pltpu.VMEM),
        scratch_shapes=[
            pltpu.VMEM((COLS, NFFT), BF16),
            pltpu.VMEM((STEPS, STATIONS * FRAMES // STEPS, NFFT), BF16),
            pltpu.VMEM((DOMS * MINE * STATIONS, LANES), F32),
            pltpu.SemaphoreType.DMA,
            pltpu.SemaphoreType.DMA((STEPS,)),
        ],
        compiler_params=pltpu.CompilerParams(vmem_limit_bytes=32 << 20),
        cost_estimate=pl.CostEstimate(
            flops=2 * COLS * NFFT * STATIONS * FRAMES, bytes_accessed=7 << 20, transcendentals=0
        ),
    )(table, volts)


def prep_kernel(map_ref, beam_ref, weight_ref, trial_ref, out_ref, turn_ref):
    section, dom = lax.axis_index("section"), lax.axis_index("dom")
    station = lax.broadcasted_iota(jnp.int32, (NSTAT, NSTAT), 0)
    chosen = jnp.where(station == map_ref[...], 1.0, 0.0).astype(BF16)
    entries = jnp.dot(
        beam_ref[...].astype(F32).astype(BF16), chosen, preferred_element_type=F32
    ).astype(jnp.int32)
    here = lax.broadcasted_iota(jnp.int32, (MINE, DOMS), 1)
    wanted = lax.broadcasted_iota(jnp.int32, (MINE, DOMS), 0) + section * MINE
    select = jnp.where(here == wanted, 1.0, 0.0).astype(BF16)
    weights = lax.dot_general(select, weight_ref[...], NT, preferred_element_type=F32)
    for j in range(MINE):
        row = jnp.broadcast_to(weights[j : j + 1, :], (BEAMS, LANES))
        for part in range(2):
            for t in range(NSTAT // LANES):
                which = entries[:, LANES * t : LANES * (t + 1)] + part * NTAB
                value = jnp.take_along_axis(row, which, axis=1)
                out_ref[j, pl.ds(part * BEAMS, BEAMS), pl.ds(LANES * t, LANES)] = value.astype(BF16)
    trial = lax.broadcasted_iota(jnp.int32, (NDM, LANES), 0)
    lane = lax.broadcasted_iota(jnp.int32, (NDM, LANES), 1)
    k = lane % FRAMES
    kappa = jnp.where(k < FRAMES // 2, k, k - FRAMES).astype(F32)
    measure = (trial + 1).astype(F32) / NDM
    column = jnp.broadcast_to(trial_ref[...].astype(F32), (BEAMS, BEAMS)).T
    onehot = jnp.where(
        column[:, :NDM] == lax.broadcasted_iota(jnp.int32, (BEAMS, NDM), 1).astype(F32), 1.0, 0.0
    )
    for j in range(MINE):
        channel = jnp.full((NDM, LANES), dom * (SECTIONS * MINE) + section * MINE + j, jnp.int32)
        freq = 1.0 + channel.astype(F32) / CH
        spread = 1.0 / (freq * freq * freq)
        phase = math.pi * measure * spread * (kappa * kappa / FRAMES)
        sine = jnp.sin(phase)
        turn_ref[0, j] = jnp.dot(
            onehot, jnp.cos(phase), precision=lax.Precision.HIGHEST, preferred_element_type=F32
        )
        turn_ref[1, j] = jnp.dot(
            onehot,
            jnp.where(lane < FRAMES, -sine, sine),
            precision=lax.Precision.HIGHEST,
            preferred_element_type=F32,
        )


def prep(station_map, beam_table, weight_table, dm_trial):
    return pl.pallas_call(
        prep_kernel,
        name="prep",
        out_shape=(
            jax.ShapeDtypeStruct((MINE, 2 * BEAMS, NSTAT), BF16),
            jax.ShapeDtypeStruct((2, MINE, BEAMS, LANES), F32),
        ),
        compiler_params=pltpu.CompilerParams(vmem_limit_bytes=32 << 20),
        cost_estimate=pl.CostEstimate(
            flops=4_000_000_000, bytes_accessed=16 << 20, transcendentals=65536
        ),
    )(
        station_map.reshape(1, NSTAT),
        beam_table,
        weight_table.reshape(2 * NTAB, weight_table.shape[2]),
        dm_trial.reshape(1, BEAMS),
    )


def split_dot(rows, high, low):
    top = rows.astype(BF16)
    rest = (rows - top.astype(F32)).astype(BF16)
    return (
        jnp.dot(top, high, preferred_element_type=F32)
        + jnp.dot(rest, high, preferred_element_type=F32)
        + jnp.dot(top, low, preferred_element_type=F32)
    )


def beam_kernel(
    signal_hbm, weight_hbm, turn_hbm, frame_ref, out_ref, signal, weight, turn, power, sems
):
    copies = []
    for j in range(MINE):
        rows = pl.ds(j * STATIONS, STATIONS)
        copies.append(
            (
                pltpu.make_async_copy(signal_hbm.at[:, rows], signal.at[j], sems.at[j, 0]),
                pltpu.make_async_copy(weight_hbm.at[j], weight.at[j], sems.at[j, 1]),
                pltpu.make_async_copy(turn_hbm.at[:, j], turn.at[j], sems.at[j, 2]),
            )
        )
    for group in copies:
        for copy in group:
            copy.start()
    low = lax.broadcasted_iota(jnp.int32, (BEAMS, LANES), 1) < FRAMES
    half = MINE // 2
    for q in range(half):
        found = []
        for j in (q, q + half):
            for copy in copies[j]:
                copy.wait()
            product = jnp.dot(
                weight[j], signal[j].reshape(NSTAT, LANES), preferred_element_type=F32
            )
            crossed = pltpu.roll(product[BEAMS:], FRAMES, 1)
            series = product[:BEAMS] + jnp.where(low, -crossed, crossed)
            bins = split_dot(series, frame_ref[0], frame_ref[1])
            rotated = bins * turn[j, 0] + pltpu.roll(bins, FRAMES, 1) * turn[j, 1]
            result = split_dot(rotated, frame_ref[2], frame_ref[3])
            square = result * result
            found.append(square + pltpu.roll(square, FRAMES, 1))
        power[pl.ds(q, BEAMS, stride=half), :] = jnp.where(low, found[0], found[1])
    out_ref[...] = power[...].astype(BF16)


def form_beams(signal, weights, turns, frames):
    return pl.pallas_call(
        beam_kernel,
        name="beams",
        out_shape=jax.ShapeDtypeStruct((BEAMS * MINE // 2, LANES), BF16),
        in_specs=[pl.BlockSpec(memory_space=pl.ANY)] * 3 + [pl.BlockSpec(memory_space=pltpu.VMEM)],
        out_specs=pl.BlockSpec(memory_space=pltpu.VMEM),
        scratch_shapes=[
            pltpu.VMEM((MINE, DOMS, STATIONS, LANES), BF16),
            pltpu.VMEM((MINE, 2 * BEAMS, NSTAT), BF16),
            pltpu.VMEM((MINE, 2, BEAMS, LANES), F32),
            pltpu.VMEM((BEAMS * MINE // 2, LANES), F32),
            pltpu.SemaphoreType.DMA((MINE, 3)),
        ],
        compiler_params=pltpu.CompilerParams(vmem_limit_bytes=32 << 20),
        cost_estimate=pl.CostEstimate(
            flops=400_000_000, bytes_accessed=4 << 20, transcendentals=0
        ),
    )(signal, weights, turns, frames)


def order_kernel(power_ref, out_ref):
    half = MINE // 2
    count = SECTIONS * DOMS * half
    channel = lax.broadcasted_iota(jnp.int32, (count, CH), 1)
    row = lax.broadcasted_iota(jnp.int32, (count, CH), 0)
    owner = channel // (SECTIONS * MINE)
    section = channel // MINE % SECTIONS
    wanted = section * (DOMS * half) + owner * half + channel % half
    place = jnp.where(row == wanted, 1.0, 0.0).astype(BF16)
    turned = power_ref[...].astype(F32).T.astype(BF16)
    placed = jnp.dot(turned, place, preferred_element_type=F32)
    high = lax.broadcasted_iota(jnp.int32, (FRAMES, CH), 1) // half % 2 == 1
    out_ref[0] = jnp.where(high, placed[FRAMES:], placed[:FRAMES])


def order(power):
    return pl.pallas_call(
        order_kernel,
        name="order",
        out_shape=jax.ShapeDtypeStruct((1, FRAMES, CH), F32),
        compiler_params=pltpu.CompilerParams(vmem_limit_bytes=32 << 20),
    )(power)


def body(voltages, station_map, beam_table, weight_table, dm_trial):
    volts = voltages.reshape(STATIONS * FRAMES, NFFT)
    spectra = channelise(jnp.asarray(dft_table()), volts)
    signal = lax.all_to_all(spectra, "dom", split_axis=0, concat_axis=0, tiled=True)
    weights, turns = prep(station_map, beam_table, weight_table, dm_trial)
    power = form_beams(signal, weights, turns, jnp.asarray(frame_tables()))
    power = power.reshape(BEAMS, MINE // 2, LANES)
    power = lax.all_to_all(power, ("section", "dom"), split_axis=0, concat_axis=0, tiled=True)
    return order(power.reshape(BEAMS * MINE // 2, LANES))


def solution(mesh):
    in_specs = (P("dom", None, None), P(), P(), P(None, None, "dom"), P())
    out_specs = P(("section", "dom"), None, None)
    return jax.shard_map(body, mesh=mesh, in_specs=in_specs, out_specs=out_specs, check_vma=False)
```

```python
import math

import jax
import jax.numpy as jnp
import ml_dtypes
import numpy as np
from jax import lax
from jax.experimental import pallas as pl
from jax.experimental.pallas import tpu as pltpu
from jax.sharding import PartitionSpec as P

NSTAT = 512
NFFT = 2048
CH = 1024
BEAMS = 128
NTAB = 64
FRAMES = 64
NDM = 32
SECTIONS = 4
DOMS = 32
STATIONS = NSTAT // DOMS
MINE = CH // (SECTIONS * DOMS)
LANES = 128
COLS = 2 * CH // SECTIONS
STEPS = 4
PIECE = NFFT // STEPS
NT = (((1,), (1,)), ((), ()))
F32 = jnp.float32
BF16 = jnp.bfloat16


def dft_table():
    sample = np.arange(NFFT)
    window = 0.5 - 0.5 * np.cos(sample.astype(np.float32) * np.float32(2.0 * math.pi / NFFT))
    scale = (window / np.float32(math.sqrt(NFFT))).astype(np.float32)
    angle = (np.arange(CH)[:, None] * sample[None, :] % NFFT).astype(np.float32) * np.float32(
        2.0 * math.pi / NFFT
    )
    parts = np.stack((np.cos(angle) * scale, -np.sin(angle) * scale))
    parts = parts.reshape(2, DOMS, SECTIONS, MINE, NFFT).transpose(2, 1, 0, 3, 4)
    return parts.reshape(SECTIONS, COLS, NFFT).astype(ml_dtypes.bfloat16)


def frame_tables():
    index = np.arange(FRAMES)
    angle = (index[:, None] * index[None, :] % FRAMES) * (2.0 * math.pi / FRAMES)
    cosine, sine = np.cos(angle), np.sin(angle)
    forward = np.block([[cosine, -sine], [sine, cosine]])
    inverse = np.block([[cosine, sine], [-sine, cosine]]) / FRAMES
    tables = []
    for table in (forward, inverse):
        high = table.astype(ml_dtypes.bfloat16)
        tables += [high, (table - high.astype(np.float64)).astype(ml_dtypes.bfloat16)]
    return np.stack(tables)


def channelise_kernel(
    table_hbm, volts_hbm, out_hbm, table, volts, total, turned, out, table_sem, volts_sem, out_sem
):
    section = lax.axis_index("section")
    pieces = [pl.ds(n * PIECE, PIECE) for n in range(STEPS)]
    loads = [
        (
            pltpu.make_async_copy(table_hbm.at[section, :, p], table.at[:, p], table_sem.at[n]),
            pltpu.make_async_copy(volts_hbm.at[:, p], volts.at[:, p], volts_sem.at[n]),
        )
        for n, p in enumerate(pieces)
    ]
    for pair in loads:
        for load in pair:
            load.start()
    for n in range(STEPS - 1):
        for load in loads[n]:
            load.wait()
        term = lax.dot_general(
            table[:, pieces[n]], volts[:, pieces[n]], NT, preferred_element_type=F32
        )
        if n == 0:
            total[...] = term
        else:
            total[...] += term
    for load in loads[-1]:
        load.wait()
    low = lax.broadcasted_iota(jnp.int32, (8, LANES), 1) < FRAMES
    for part in range(2):
        rows = pl.ds(part * COLS // 2, COLS // 2)
        spectrum = total[rows, :] + lax.dot_general(
            table[rows, pieces[-1]], volts[:, pieces[-1]], NT, preferred_element_type=F32
        )
        for d in range(DOMS // 2):
            for t in range(STATIONS // 2):
                real = spectrum[16 * d : 16 * d + 8, LANES * t : LANES * (t + 1)]
                imag = spectrum[16 * d + 8 : 16 * d + 16, LANES * t : LANES * (t + 1)]
                base = (part * DOMS // 2 + d) * MINE * STATIONS + 2 * t
                turned[pl.ds(base, 8, stride=STATIONS), :] = jnp.where(
                    low, real, pltpu.roll(imag, FRAMES, 1)
                )
                turned[pl.ds(base + 1, 8, stride=STATIONS), :] = jnp.where(
                    low, pltpu.roll(real, FRAMES, 1), imag
                )
    stores = []
    for part in range(2):
        half = pl.ds(part * DOMS // 2, DOMS // 2)
        for d in range(part * DOMS // 2, (part + 1) * DOMS // 2):
            out[d] = turned[pl.ds(d * LANES, LANES), :].astype(BF16)
        stores.append(pltpu.make_async_copy(out.at[half], out_hbm.at[half], out_sem.at[part]))
        stores[-1].start()
    for store in stores:
        store.wait()


def channelise(table, volts):
    return pl.pallas_call(
        channelise_kernel,
        name="channelise",
        out_shape=jax.ShapeDtypeStruct((DOMS, MINE * STATIONS, LANES), BF16),
        in_specs=[pl.BlockSpec(memory_space=pl.ANY)] * 2,
        out_specs=pl.BlockSpec(memory_space=pl.ANY),
        scratch_shapes=[
            pltpu.VMEM((COLS, NFFT), BF16),
            pltpu.VMEM((STATIONS * FRAMES, NFFT), BF16),
            pltpu.VMEM((COLS, STATIONS * FRAMES), F32),
            pltpu.VMEM((DOMS * MINE * STATIONS, LANES), F32),
            pltpu.VMEM((DOMS, MINE * STATIONS, LANES), BF16),
            pltpu.SemaphoreType.DMA((STEPS,)),
            pltpu.SemaphoreType.DMA((STEPS,)),
            pltpu.SemaphoreType.DMA((2,)),
        ],
        compiler_params=pltpu.CompilerParams(vmem_limit_bytes=61 << 20),
        cost_estimate=pl.CostEstimate(
            flops=2 * COLS * NFFT * STATIONS * FRAMES, bytes_accessed=7 << 20, transcendentals=0
        ),
    )(table, volts)


def prep_kernel(map_ref, beam_ref, weight_ref, out_ref, turn_ref):
    section, dom = lax.axis_index("section"), lax.axis_index("dom")
    station = lax.broadcasted_iota(jnp.int32, (NSTAT, NSTAT), 0)
    chosen = jnp.where(station == map_ref[...], 1.0, 0.0).astype(BF16)
    entries = jnp.dot(
        beam_ref[...].astype(F32).astype(BF16), chosen, preferred_element_type=F32
    ).astype(jnp.int32)
    here = lax.broadcasted_iota(jnp.int32, (MINE, DOMS), 1)
    wanted = lax.broadcasted_iota(jnp.int32, (MINE, DOMS), 0) + section * MINE
    select = jnp.where(here == wanted, 1.0, 0.0).astype(BF16)
    weights = lax.dot_general(select, weight_ref[...], NT, preferred_element_type=F32)
    for j in range(MINE):
        row = jnp.broadcast_to(weights[j : j + 1, :], (BEAMS, LANES))
        for part in range(2):
            for t in range(NSTAT // LANES):
                which = entries[:, LANES * t : LANES * (t + 1)] + part * NTAB
                value = jnp.take_along_axis(row, which, axis=1)
                out_ref[j, pl.ds(part * BEAMS, BEAMS), pl.ds(LANES * t, LANES)] = value.astype(BF16)
    trial = lax.broadcasted_iota(jnp.int32, (NDM, LANES), 0)
    lane = lax.broadcasted_iota(jnp.int32, (NDM, LANES), 1)
    k = lane % FRAMES
    kappa = jnp.where(k < FRAMES // 2, k, k - FRAMES).astype(F32)
    measure = (trial + 1).astype(F32) / NDM
    for j in range(MINE):
        channel = jnp.full((NDM, LANES), dom * (SECTIONS * MINE) + section * MINE + j, jnp.int32)
        freq = 1.0 + channel.astype(F32) / CH
        spread = 1.0 / (freq * freq * freq)
        phase = math.pi * measure * spread * (kappa * kappa / FRAMES)
        sine = jnp.sin(phase)
        tables = []
        for table in (jnp.cos(phase), jnp.where(lane < FRAMES, -sine, sine)):
            top = table.astype(BF16)
            tables += [top, (table - top.astype(F32)).astype(BF16)]
        turn_ref[j] = jnp.concatenate(tables, axis=1)


def prep(station_map, beam_table, weight_table):
    return pl.pallas_call(
        prep_kernel,
        name="prep",
        out_shape=(
            jax.ShapeDtypeStruct((MINE, 2 * BEAMS, NSTAT), BF16),
            jax.ShapeDtypeStruct((MINE, NDM, 4 * LANES), BF16),
        ),
        compiler_params=pltpu.CompilerParams(vmem_limit_bytes=32 << 20),
        cost_estimate=pl.CostEstimate(
            flops=4_000_000_000, bytes_accessed=16 << 20, transcendentals=65536
        ),
    )(
        station_map.reshape(1, NSTAT),
        beam_table,
        weight_table.reshape(2 * NTAB, weight_table.shape[2]),
    )


def split_dot(rows, high, low):
    top = rows.astype(BF16)
    rest = (rows - top.astype(F32)).astype(BF16)
    return (
        jnp.dot(top, high, preferred_element_type=F32)
        + jnp.dot(rest, high, preferred_element_type=F32)
        + jnp.dot(top, low, preferred_element_type=F32)
    )


def beam_kernel(signal_ref, weight_ref, turn_ref, trial_ref, frame_ref, out_ref, series, power):
    column = jnp.broadcast_to(trial_ref[...].astype(F32), (BEAMS, BEAMS)).T[:, :NDM]
    trial = lax.broadcasted_iota(jnp.int32, (BEAMS, NDM), 1).astype(F32)
    onehot = jnp.where(column == trial, 1.0, 0.0).astype(BF16)
    low = lax.broadcasted_iota(jnp.int32, (BEAMS, LANES), 1) < FRAMES
    for j in range(MINE):
        signal = signal_ref[:, pl.ds(j * STATIONS, STATIONS), :].reshape(NSTAT, LANES)
        product = jnp.dot(weight_ref[j], signal, preferred_element_type=F32)
        crossed = pltpu.roll(product[BEAMS:], FRAMES, 1)
        series[pl.ds(j * BEAMS, BEAMS), :] = product[:BEAMS] + jnp.where(low, -crossed, crossed)
    half = MINE // 2
    bins = split_dot(series[...], frame_ref[0], frame_ref[1])
    turns = [jnp.dot(onehot, turn_ref[j], preferred_element_type=F32) for j in range(MINE)]
    turn = jnp.concatenate(turns, axis=0)
    direct = turn[:, :LANES] + turn[:, LANES : 2 * LANES]
    across = turn[:, 2 * LANES : 3 * LANES] + turn[:, 3 * LANES :]
    rotated = bins * direct + pltpu.roll(bins, FRAMES, 1) * across
    result = split_dot(rotated, frame_ref[2], frame_ref[3])
    square = result * result
    found = square + pltpu.roll(square, FRAMES, 1)
    for q in range(half):
        power[pl.ds(q, BEAMS, stride=half), :] = jnp.where(
            low,
            found[q * BEAMS : (q + 1) * BEAMS],
            found[(q + half) * BEAMS : (q + half + 1) * BEAMS],
        )
    out_ref[...] = power[...].astype(BF16)


def form_beams(signal, weights, turns, dm_trial, frames):
    return pl.pallas_call(
        beam_kernel,
        name="beams",
        out_shape=jax.ShapeDtypeStruct((BEAMS * MINE // 2, LANES), BF16),
        scratch_shapes=[
            pltpu.VMEM((MINE * BEAMS, LANES), F32),
            pltpu.VMEM((BEAMS * MINE // 2, LANES), F32),
        ],
        compiler_params=pltpu.CompilerParams(vmem_limit_bytes=24 << 20),
        cost_estimate=pl.CostEstimate(
            flops=400_000_000, bytes_accessed=4 << 20, transcendentals=0
        ),
    )(signal, weights, turns, dm_trial.reshape(1, BEAMS), frames)


def order_kernel(power_ref, out_ref):
    half = MINE // 2
    count = SECTIONS * DOMS * half
    channel = lax.broadcasted_iota(jnp.int32, (count, CH), 1)
    row = lax.broadcasted_iota(jnp.int32, (count, CH), 0)
    owner = channel // (SECTIONS * MINE)
    section = channel // MINE % SECTIONS
    wanted = section * (DOMS * half) + owner * half + channel % half
    place = jnp.where(row == wanted, 1.0, 0.0).astype(BF16)
    turned = power_ref[...].astype(F32).T.astype(BF16)
    placed = jnp.dot(turned, place, preferred_element_type=F32)
    high = lax.broadcasted_iota(jnp.int32, (FRAMES, CH), 1) // half % 2 == 1
    out_ref[0] = jnp.where(high, placed[FRAMES:], placed[:FRAMES])


def order(power):
    return pl.pallas_call(
        order_kernel,
        name="order",
        out_shape=jax.ShapeDtypeStruct((1, FRAMES, CH), F32),
        compiler_params=pltpu.CompilerParams(vmem_limit_bytes=32 << 20),
    )(power)


def body(voltages, station_map, beam_table, weight_table, dm_trial):
    volts = voltages.reshape(STATIONS * FRAMES, NFFT)
    spectra = channelise(jnp.asarray(dft_table()), volts)
    signal = lax.all_to_all(spectra, "dom", split_axis=0, concat_axis=0, tiled=True)
    weights, turns = prep(station_map, beam_table, weight_table)
    power = form_beams(signal, weights, turns, dm_trial, jnp.asarray(frame_tables()))
    power = power.reshape(BEAMS, MINE // 2, LANES)
    power = lax.all_to_all(power, ("section", "dom"), split_axis=0, concat_axis=0, tiled=True)
    return order(power.reshape(BEAMS * MINE // 2, LANES))


def solution(mesh):
    in_specs = (P("dom", None, None), P(), P(), P(None, None, "dom"), P())
    out_specs = P(("section", "dom"), None, None)
    return jax.shard_map(body, mesh=mesh, in_specs=in_specs, out_specs=out_specs, check_vma=False)
```

```python
import math

import jax
import jax.numpy as jnp
import ml_dtypes
import numpy as np
from jax import lax
from jax.experimental import pallas as pl
from jax.experimental.pallas import tpu as pltpu
from jax.sharding import PartitionSpec as P

NSTAT = 512
NFFT = 2048
CH = 1024
BEAMS = 128
NTAB = 64
FRAMES = 64
NDM = 32
SECTIONS = 4
DOMS = 32
STATIONS = NSTAT // DOMS
MINE = CH // (SECTIONS * DOMS)
LANES = 128
COLS = 2 * CH // SECTIONS
STEPS = 4
PIECE = NFFT // STEPS
NT = (((1,), (1,)), ((), ()))
F32 = jnp.float32
BF16 = jnp.bfloat16


def dft_table():
    sample = np.arange(NFFT)
    window = 0.5 - 0.5 * np.cos(sample.astype(np.float32) * np.float32(2.0 * math.pi / NFFT))
    scale = (window / np.float32(math.sqrt(NFFT))).astype(np.float32)
    angle = (np.arange(CH)[:, None] * sample[None, :] % NFFT).astype(np.float32) * np.float32(
        2.0 * math.pi / NFFT
    )
    parts = np.stack((np.cos(angle) * scale, -np.sin(angle) * scale))
    parts = parts.reshape(2, DOMS, SECTIONS, MINE, NFFT).transpose(2, 1, 0, 3, 4)
    return parts.reshape(SECTIONS, COLS, NFFT).astype(ml_dtypes.bfloat16)


def frame_table():
    index = np.arange(FRAMES)
    angle = (index[:, None] * index[None, :] % FRAMES) * (2.0 * math.pi / FRAMES)
    cosine, sine = np.cos(angle), np.sin(angle)
    table = np.block([[cosine, -sine], [sine, cosine]])
    high = table.astype(ml_dtypes.bfloat16)
    return np.stack((high, (table - high.astype(np.float64)).astype(ml_dtypes.bfloat16)))


def channelise_kernel(
    table_hbm, volts_hbm, out_hbm, table, volts, total, turned, out, table_sem, volts_sem, out_sem
):
    section = lax.axis_index("section")
    pieces = [pl.ds(n * PIECE, PIECE) for n in range(STEPS)]
    loads = [
        (
            pltpu.make_async_copy(table_hbm.at[section, :, p], table.at[:, p], table_sem.at[n]),
            pltpu.make_async_copy(volts_hbm.at[:, p], volts.at[:, p], volts_sem.at[n]),
        )
        for n, p in enumerate(pieces)
    ]
    for pair in loads:
        for load in pair:
            load.start()
    for n in range(STEPS - 1):
        for load in loads[n]:
            load.wait()
        term = lax.dot_general(
            table[:, pieces[n]], volts[:, pieces[n]], NT, preferred_element_type=F32
        )
        if n == 0:
            total[...] = term
        else:
            total[...] += term
    for load in loads[-1]:
        load.wait()
    low = lax.broadcasted_iota(jnp.int32, (8, LANES), 1) < FRAMES
    for part in range(2):
        rows = pl.ds(part * COLS // 2, COLS // 2)
        spectrum = total[rows, :] + lax.dot_general(
            table[rows, pieces[-1]], volts[:, pieces[-1]], NT, preferred_element_type=F32
        )
        for d in range(DOMS // 2):
            for t in range(STATIONS // 2):
                real = spectrum[16 * d : 16 * d + 8, LANES * t : LANES * (t + 1)]
                imag = spectrum[16 * d + 8 : 16 * d + 16, LANES * t : LANES * (t + 1)]
                base = (part * DOMS // 2 + d) * MINE * STATIONS + 2 * t
                turned[pl.ds(base, 8, stride=STATIONS), :] = jnp.where(
                    low, real, pltpu.roll(imag, FRAMES, 1)
                )
                turned[pl.ds(base + 1, 8, stride=STATIONS), :] = jnp.where(
                    low, pltpu.roll(real, FRAMES, 1), imag
                )
    stores = []
    for part in range(2):
        half = pl.ds(part * DOMS // 2, DOMS // 2)
        for d in range(part * DOMS // 2, (part + 1) * DOMS // 2):
            out[d] = turned[pl.ds(d * LANES, LANES), :].astype(BF16)
        stores.append(pltpu.make_async_copy(out.at[half], out_hbm.at[half], out_sem.at[part]))
        stores[-1].start()
    for store in stores:
        store.wait()


def channelise(table, volts):
    return pl.pallas_call(
        channelise_kernel,
        name="channelise",
        out_shape=jax.ShapeDtypeStruct((DOMS, MINE * STATIONS, LANES), BF16),
        in_specs=[pl.BlockSpec(memory_space=pl.ANY)] * 2,
        out_specs=pl.BlockSpec(memory_space=pl.ANY),
        scratch_shapes=[
            pltpu.VMEM((COLS, NFFT), BF16),
            pltpu.VMEM((STATIONS * FRAMES, NFFT), BF16),
            pltpu.VMEM((COLS, STATIONS * FRAMES), F32),
            pltpu.VMEM((DOMS * MINE * STATIONS, LANES), F32),
            pltpu.VMEM((DOMS, MINE * STATIONS, LANES), BF16),
            pltpu.SemaphoreType.DMA((STEPS,)),
            pltpu.SemaphoreType.DMA((STEPS,)),
            pltpu.SemaphoreType.DMA((2,)),
        ],
        compiler_params=pltpu.CompilerParams(vmem_limit_bytes=61 << 20),
        cost_estimate=pl.CostEstimate(
            flops=2 * COLS * NFFT * STATIONS * FRAMES, bytes_accessed=7 << 20, transcendentals=0
        ),
    )(table, volts)


def prep_kernel(map_ref, beam_ref, weight_ref, trial_ref, out_ref, turn_ref, choice_ref):
    section, dom = lax.axis_index("section"), lax.axis_index("dom")
    place = lax.broadcasted_iota(jnp.int32, (BEAMS, BEAMS), 0)
    beam = lax.broadcasted_iota(jnp.int32, (BEAMS, BEAMS), 1)
    swap = jnp.where(beam == place % SECTIONS * DOMS + place // SECTIONS, 1.0, 0.0).astype(BF16)
    station = lax.broadcasted_iota(jnp.int32, (NSTAT, NSTAT), 0)
    chosen = jnp.where(station == map_ref[...], 1.0, 0.0).astype(BF16)
    swapped = jnp.dot(swap, beam_ref[...].astype(F32).astype(BF16), preferred_element_type=F32)
    entries = jnp.dot(swapped.astype(BF16), chosen, preferred_element_type=F32).astype(jnp.int32)
    wanted = lax.broadcasted_iota(jnp.int32, (2 * NDM, BEAMS), 0) % NDM
    onehot = jnp.where(wanted == trial_ref[...], 1.0, 0.0).astype(BF16)
    choice_ref[...] = lax.dot_general(swap, onehot, NT, preferred_element_type=F32).astype(BF16)
    here = lax.broadcasted_iota(jnp.int32, (MINE, DOMS), 1)
    wanted = lax.broadcasted_iota(jnp.int32, (MINE, DOMS), 0) + section * MINE
    select = jnp.where(here == wanted, 1.0, 0.0).astype(BF16)
    weights = lax.dot_general(select, weight_ref[...], NT, preferred_element_type=F32)
    for j in range(MINE):
        row = jnp.broadcast_to(weights[j : j + 1, :], (BEAMS, LANES))
        for part in range(2):
            for t in range(NSTAT // LANES):
                which = entries[:, LANES * t : LANES * (t + 1)] + part * NTAB
                value = jnp.take_along_axis(row, which, axis=1)
                out_ref[j, pl.ds(part * BEAMS, BEAMS), pl.ds(LANES * t, LANES)] = value.astype(BF16)
    trial = lax.broadcasted_iota(jnp.int32, (NDM, LANES), 0)
    lane = lax.broadcasted_iota(jnp.int32, (NDM, LANES), 1)
    k = lane % FRAMES
    kappa = jnp.where(k < FRAMES // 2, k, k - FRAMES).astype(F32)
    measure = (trial + 1).astype(F32) / NDM
    for j in range(MINE):
        channel = jnp.full((NDM, LANES), dom * (SECTIONS * MINE) + section * MINE + j, jnp.int32)
        freq = 1.0 + channel.astype(F32) / CH
        spread = 1.0 / (freq * freq * freq)
        phase = math.pi * measure * spread * (kappa * kappa / FRAMES)
        sine = jnp.sin(phase)
        table = jnp.concatenate((jnp.cos(phase), jnp.where(lane < FRAMES, -sine, sine)), axis=1)
        top = table.astype(BF16)
        turn_ref[j, :NDM] = top
        turn_ref[j, NDM:] = (table - top.astype(F32)).astype(BF16)


def prep(station_map, beam_table, weight_table, dm_trial):
    return pl.pallas_call(
        prep_kernel,
        name="prep",
        out_shape=(
            jax.ShapeDtypeStruct((MINE, 2 * BEAMS, NSTAT), BF16),
            jax.ShapeDtypeStruct((MINE, 2 * NDM, 2 * LANES), BF16),
            jax.ShapeDtypeStruct((BEAMS, 2 * NDM), BF16),
        ),
        compiler_params=pltpu.CompilerParams(vmem_limit_bytes=32 << 20),
        cost_estimate=pl.CostEstimate(
            flops=4_000_000_000, bytes_accessed=16 << 20, transcendentals=65536
        ),
    )(
        station_map.reshape(1, NSTAT),
        beam_table,
        weight_table.reshape(2 * NTAB, weight_table.shape[2]),
        dm_trial.reshape(1, BEAMS),
    )


def split_dot(rows, high, low, turned):
    top = rows.astype(BF16)
    rest = (rows - top.astype(F32)).astype(BF16)
    side = int(turned)
    tables = jnp.concatenate(
        (
            jnp.concatenate((high, low), axis=1 - side),
            jnp.concatenate((high, jnp.zeros_like(high)), axis=1 - side),
        ),
        axis=side,
    )
    both = lax.dot_general(
        jnp.concatenate((top, rest), axis=1),
        tables,
        (((1,), (side,)), ((), ())),
        preferred_element_type=F32,
    )
    return both[:, :LANES] + both[:, LANES:]


def beam_kernel(signal_ref, weight_ref, turn_ref, choice_ref, frame_ref, out_ref, series, power):
    low = lax.broadcasted_iota(jnp.int32, (BEAMS, LANES), 1) < FRAMES
    for j in range(MINE):
        signal = signal_ref[:, pl.ds(j * STATIONS, STATIONS), :].reshape(NSTAT, LANES)
        product = jnp.dot(weight_ref[j], signal, preferred_element_type=F32)
        crossed = pltpu.roll(product[BEAMS:], FRAMES, 1)
        series[pl.ds(j * BEAMS, BEAMS), :] = product[:BEAMS] + jnp.where(low, -crossed, crossed)
    half = MINE // 2
    bins = split_dot(series[...], frame_ref[0], frame_ref[1], False)
    choice = choice_ref[...]
    turns = [jnp.dot(choice, turn_ref[j], preferred_element_type=F32) for j in range(MINE)]
    turn = jnp.concatenate(turns, axis=0)
    rotated = bins * turn[:, :LANES] + pltpu.roll(bins, FRAMES, 1) * turn[:, LANES:]
    result = split_dot(rotated, frame_ref[0], frame_ref[1], True) * (1.0 / FRAMES)
    square = result * result
    found = square + pltpu.roll(square, FRAMES, 1)
    for q in range(half):
        power[pl.ds(q, BEAMS, stride=half), :] = jnp.where(
            low,
            found[q * BEAMS : (q + 1) * BEAMS],
            found[(q + half) * BEAMS : (q + half + 1) * BEAMS],
        )
    out_ref[...] = power[...].astype(BF16)


def form_beams(signal, weights, turns, choice, frames):
    return pl.pallas_call(
        beam_kernel,
        name="beams",
        out_shape=jax.ShapeDtypeStruct((BEAMS * MINE // 2, LANES), BF16),
        scratch_shapes=[
            pltpu.VMEM((MINE * BEAMS, LANES), F32),
            pltpu.VMEM((BEAMS * MINE // 2, LANES), F32),
        ],
        compiler_params=pltpu.CompilerParams(vmem_limit_bytes=24 << 20),
        cost_estimate=pl.CostEstimate(
            flops=400_000_000, bytes_accessed=4 << 20, transcendentals=0
        ),
    )(signal, weights, turns, choice, frames)


def order_kernel(power_ref, out_ref):
    half = MINE // 2
    row = lax.broadcasted_iota(jnp.int32, (LANES, 2 * LANES), 0)
    channel = lax.broadcasted_iota(jnp.int32, (1, 2 * LANES), 1)
    place = jnp.where(row == channel // MINE * half + channel % half, 1.0, 0.0).astype(BF16)
    high = lax.broadcasted_iota(jnp.int32, (FRAMES, 2 * LANES), 1) // half % 2 == 1
    for n in range(CH // (2 * LANES)):
        rows = power_ref[pl.ds(n * LANES, LANES), :]
        placed = lax.dot_general(
            rows, place, (((0,), (0,)), ((), ())), preferred_element_type=F32
        )
        out_ref[0, :, pl.ds(n * 2 * LANES, 2 * LANES)] = jnp.where(
            high, placed[FRAMES:], placed[:FRAMES]
        )


def order(power):
    return pl.pallas_call(
        order_kernel,
        name="order",
        out_shape=jax.ShapeDtypeStruct((1, FRAMES, CH), F32),
        compiler_params=pltpu.CompilerParams(vmem_limit_bytes=32 << 20),
    )(power)


def body(voltages, station_map, beam_table, weight_table, dm_trial):
    volts = voltages.reshape(STATIONS * FRAMES, NFFT)
    spectra = channelise(jnp.asarray(dft_table()), volts)
    signal = lax.all_to_all(spectra, "dom", split_axis=0, concat_axis=0, tiled=True)
    weights, turns, choice = prep(station_map, beam_table, weight_table, dm_trial)
    power = form_beams(signal, weights, turns, choice, jnp.asarray(frame_table()))
    power = power.reshape(BEAMS, MINE // 2, LANES)
    power = lax.all_to_all(power, ("dom", "section"), split_axis=0, concat_axis=0, tiled=True)
    return order(power.reshape(BEAMS * MINE // 2, LANES))


def solution(mesh):
    in_specs = (P("dom", None, None), P(), P(), P(None, None, "dom"), P())
    out_specs = P(("section", "dom"), None, None)
    return jax.shard_map(body, mesh=mesh, in_specs=in_specs, out_specs=out_specs, check_vma=False)
```

```python
import math

import jax
import jax.numpy as jnp
import ml_dtypes
import numpy as np
from jax import lax
from jax.experimental import pallas as pl
from jax.experimental.pallas import tpu as pltpu
from jax.sharding import PartitionSpec as P

NSTAT = 512
NFFT = 2048
CH = 1024
BEAMS = 128
NTAB = 64
FRAMES = 64
NDM = 32
SECTIONS = 4
DOMS = 32
STATIONS = NSTAT // DOMS
MINE = CH // (SECTIONS * DOMS)
LANES = 128
COLS = 2 * CH // SECTIONS
SHARE = SECTIONS * MINE // 2
STEPS = 4
PIECE = NFFT // STEPS
NT = (((1,), (1,)), ((), ()))
GRID = (4, 4, 2)
PARTNERS = [int(d) for d in np.arange(DOMS).reshape(GRID).transpose(2, 1, 0).ravel()]
EVERYONE = [s * DOMS + d for d in PARTNERS for s in range(SECTIONS)]
F32 = jnp.float32
BF16 = jnp.bfloat16


def dft_table():
    sample = np.arange(NFFT)
    window = 0.5 - 0.5 * np.cos(sample.astype(np.float32) * np.float32(2.0 * math.pi / NFFT))
    scale = (window / np.float32(math.sqrt(NFFT))).astype(np.float32)
    angle = (np.arange(CH)[:, None] * sample[None, :] % NFFT).astype(np.float32) * np.float32(
        2.0 * math.pi / NFFT
    )
    parts = np.stack((np.cos(angle) * scale, -np.sin(angle) * scale))
    parts = parts.reshape(2, DOMS, SECTIONS, MINE, NFFT)[:, PARTNERS].transpose(2, 1, 0, 3, 4)
    return parts.reshape(SECTIONS, COLS, NFFT).astype(ml_dtypes.bfloat16)


def frame_table():
    index = np.arange(FRAMES)
    angle = (index[:, None] * index[None, :] % FRAMES) * (2.0 * math.pi / FRAMES)
    cosine, sine = np.cos(angle), np.sin(angle)
    table = np.block([[cosine, -sine], [sine, cosine]])
    high = table.astype(ml_dtypes.bfloat16)
    return np.stack((high, (table - high.astype(np.float64)).astype(ml_dtypes.bfloat16)))


def channelise_kernel(
    table_hbm, volts_hbm, out_hbm, table, volts, total, turned, out, table_sem, volts_sem, out_sem
):
    section = lax.axis_index("section")
    pieces = [pl.ds(n * PIECE, PIECE) for n in range(STEPS)]
    loads = [
        (
            pltpu.make_async_copy(table_hbm.at[section, :, p], table.at[:, p], table_sem.at[n]),
            pltpu.make_async_copy(volts_hbm.at[:, p], volts.at[:, p], volts_sem.at[n]),
        )
        for n, p in enumerate(pieces)
    ]
    for pair in loads:
        for load in pair:
            load.start()
    for n in range(STEPS - 1):
        for load in loads[n]:
            load.wait()
        term = lax.dot_general(
            table[:, pieces[n]], volts[:, pieces[n]], NT, preferred_element_type=F32
        )
        if n == 0:
            total[...] = term
        else:
            total[...] += term
    for load in loads[-1]:
        load.wait()
    low = lax.broadcasted_iota(jnp.int32, (8, LANES), 1) < FRAMES
    for part in range(2):
        rows = pl.ds(part * COLS // 2, COLS // 2)
        spectrum = total[rows, :] + lax.dot_general(
            table[rows, pieces[-1]], volts[:, pieces[-1]], NT, preferred_element_type=F32
        )
        for d in range(DOMS // 2):
            for t in range(STATIONS // 2):
                real = spectrum[16 * d : 16 * d + 8, LANES * t : LANES * (t + 1)]
                imag = spectrum[16 * d + 8 : 16 * d + 16, LANES * t : LANES * (t + 1)]
                base = (part * DOMS // 2 + d) * MINE * STATIONS + 2 * t
                turned[pl.ds(base, 8, stride=STATIONS), :] = jnp.where(
                    low, real, pltpu.roll(imag, FRAMES, 1)
                )
                turned[pl.ds(base + 1, 8, stride=STATIONS), :] = jnp.where(
                    low, pltpu.roll(real, FRAMES, 1), imag
                )
    stores = []
    for part in range(2):
        half = pl.ds(part * DOMS // 2, DOMS // 2)
        for d in range(part * DOMS // 2, (part + 1) * DOMS // 2):
            out[d] = turned[pl.ds(d * LANES, LANES), :].astype(BF16)
        stores.append(pltpu.make_async_copy(out.at[half], out_hbm.at[half], out_sem.at[part]))
        stores[-1].start()
    for store in stores:
        store.wait()


def channelise(table, volts):
    return pl.pallas_call(
        channelise_kernel,
        name="channelise",
        out_shape=jax.ShapeDtypeStruct((DOMS, MINE * STATIONS, LANES), BF16),
        in_specs=[pl.BlockSpec(memory_space=pl.ANY)] * 2,
        out_specs=pl.BlockSpec(memory_space=pl.ANY),
        scratch_shapes=[
            pltpu.VMEM((COLS, NFFT), BF16),
            pltpu.VMEM((STATIONS * FRAMES, NFFT), BF16),
            pltpu.VMEM((COLS, STATIONS * FRAMES), F32),
            pltpu.VMEM((DOMS * MINE * STATIONS, LANES), F32),
            pltpu.VMEM((DOMS, MINE * STATIONS, LANES), BF16),
            pltpu.SemaphoreType.DMA((STEPS,)),
            pltpu.SemaphoreType.DMA((STEPS,)),
            pltpu.SemaphoreType.DMA((2,)),
        ],
        compiler_params=pltpu.CompilerParams(vmem_limit_bytes=61 << 20),
        cost_estimate=pl.CostEstimate(
            flops=2 * COLS * NFFT * STATIONS * FRAMES, bytes_accessed=7 << 20, transcendentals=0
        ),
    )(table, volts)


def prep_kernel(map_ref, beam_ref, weight_ref, trial_ref, out_ref, turn_ref, choice_ref):
    section, dom = lax.axis_index("section"), lax.axis_index("dom")
    place = lax.broadcasted_iota(jnp.int32, (BEAMS, BEAMS), 0)
    beam = lax.broadcasted_iota(jnp.int32, (BEAMS, BEAMS), 1)
    z, y, x = place // 4 % 4, place // 16 % 4, place // 64
    owner = place % SECTIONS * DOMS + (z * 4 + y) * 2 + x
    swap = jnp.where(beam == owner, 1.0, 0.0).astype(BF16)
    station = lax.broadcasted_iota(jnp.int32, (NSTAT, NSTAT), 0)
    chosen = jnp.where(station == map_ref[...], 1.0, 0.0).astype(BF16)
    swapped = jnp.dot(swap, beam_ref[...].astype(F32).astype(BF16), preferred_element_type=F32)
    entries = jnp.dot(swapped.astype(BF16), chosen, preferred_element_type=F32).astype(jnp.int32)
    wanted = lax.broadcasted_iota(jnp.int32, (2 * NDM, BEAMS), 0) % NDM
    onehot = jnp.where(wanted == trial_ref[...], 1.0, 0.0).astype(BF16)
    choice_ref[...] = lax.dot_general(swap, onehot, NT, preferred_element_type=F32).astype(BF16)
    here = lax.broadcasted_iota(jnp.int32, (MINE, DOMS), 1)
    wanted = lax.broadcasted_iota(jnp.int32, (MINE, DOMS), 0) + section * MINE
    select = jnp.where(here == wanted, 1.0, 0.0).astype(BF16)
    weights = lax.dot_general(select, weight_ref[...], NT, preferred_element_type=F32)
    for j in range(MINE):
        row = jnp.broadcast_to(weights[j : j + 1, :], (BEAMS, LANES))
        for part in range(2):
            for t in range(NSTAT // LANES):
                which = entries[:, LANES * t : LANES * (t + 1)] + part * NTAB
                value = jnp.take_along_axis(row, which, axis=1)
                out_ref[j, pl.ds(part * BEAMS, BEAMS), pl.ds(LANES * t, LANES)] = value.astype(BF16)
    trial = lax.broadcasted_iota(jnp.int32, (NDM, LANES), 0)
    lane = lax.broadcasted_iota(jnp.int32, (NDM, LANES), 1)
    k = lane % FRAMES
    kappa = jnp.where(k < FRAMES // 2, k, k - FRAMES).astype(F32)
    measure = (trial + 1).astype(F32) / NDM
    for j in range(MINE):
        channel = jnp.full((NDM, LANES), dom * (SECTIONS * MINE) + section * MINE + j, jnp.int32)
        freq = 1.0 + channel.astype(F32) / CH
        spread = 1.0 / (freq * freq * freq)
        phase = math.pi * measure * spread * (kappa * kappa / FRAMES)
        sine = jnp.sin(phase)
        table = jnp.concatenate((jnp.cos(phase), jnp.where(lane < FRAMES, -sine, sine)), axis=1)
        top = table.astype(BF16)
        turn_ref[j, :NDM] = top
        turn_ref[j, NDM:] = (table - top.astype(F32)).astype(BF16)


def prep(station_map, beam_table, weight_table, dm_trial):
    return pl.pallas_call(
        prep_kernel,
        name="prep",
        out_shape=(
            jax.ShapeDtypeStruct((MINE, 2 * BEAMS, NSTAT), BF16),
            jax.ShapeDtypeStruct((MINE, 2 * NDM, 2 * LANES), BF16),
            jax.ShapeDtypeStruct((BEAMS, 2 * NDM), BF16),
        ),
        compiler_params=pltpu.CompilerParams(vmem_limit_bytes=32 << 20),
        cost_estimate=pl.CostEstimate(
            flops=4_000_000_000, bytes_accessed=16 << 20, transcendentals=65536
        ),
    )(
        station_map.reshape(*GRID, STATIONS).transpose(2, 1, 0, 3).reshape(1, NSTAT),
        beam_table,
        weight_table.reshape(2 * NTAB, weight_table.shape[2]),
        dm_trial.reshape(1, BEAMS),
    )


def split_dot(rows, high, low, turned):
    top = rows.astype(BF16)
    rest = (rows - top.astype(F32)).astype(BF16)
    side = int(turned)
    tables = jnp.concatenate(
        (
            jnp.concatenate((high, low), axis=1 - side),
            jnp.concatenate((high, jnp.zeros_like(high)), axis=1 - side),
        ),
        axis=side,
    )
    both = lax.dot_general(
        jnp.concatenate((top, rest), axis=1),
        tables,
        (((1,), (side,)), ((), ())),
        preferred_element_type=F32,
    )
    return both[:, :LANES] + both[:, LANES:]


def beam_kernel(signal_ref, weight_ref, turn_ref, choice_ref, frame_ref, out_ref, series, power):
    low = lax.broadcasted_iota(jnp.int32, (BEAMS, LANES), 1) < FRAMES
    for j in range(MINE):
        signal = signal_ref[:, pl.ds(j * STATIONS, STATIONS), :].reshape(NSTAT, LANES)
        product = jnp.dot(weight_ref[j], signal, preferred_element_type=F32)
        crossed = pltpu.roll(product[BEAMS:], FRAMES, 1)
        series[pl.ds(j * BEAMS, BEAMS), :] = product[:BEAMS] + jnp.where(low, -crossed, crossed)
    half = MINE // 2
    bins = split_dot(series[...], frame_ref[0], frame_ref[1], False)
    choice = choice_ref[...]
    turns = [jnp.dot(choice, turn_ref[j], preferred_element_type=F32) for j in range(MINE)]
    turn = jnp.concatenate(turns, axis=0)
    rotated = bins * turn[:, :LANES] + pltpu.roll(bins, FRAMES, 1) * turn[:, LANES:]
    result = split_dot(rotated, frame_ref[0], frame_ref[1], True) * (1.0 / FRAMES)
    square = result * result
    found = square + pltpu.roll(square, FRAMES, 1)
    for q in range(half):
        power[pl.ds(q, BEAMS, stride=half), :] = jnp.where(
            low,
            found[q * BEAMS : (q + 1) * BEAMS],
            found[(q + half) * BEAMS : (q + half + 1) * BEAMS],
        )
    out_ref[...] = power[...].astype(BF16)


def form_beams(signal, weights, turns, choice, frames):
    return pl.pallas_call(
        beam_kernel,
        name="beams",
        out_shape=jax.ShapeDtypeStruct((BEAMS * MINE // 2, LANES), BF16),
        scratch_shapes=[
            pltpu.VMEM((MINE * BEAMS, LANES), F32),
            pltpu.VMEM((BEAMS * MINE // 2, LANES), F32),
        ],
        compiler_params=pltpu.CompilerParams(vmem_limit_bytes=24 << 20),
        cost_estimate=pl.CostEstimate(
            flops=400_000_000, bytes_accessed=4 << 20, transcendentals=0
        ),
    )(signal, weights, turns, choice, frames)


def order_kernel(power_ref, out_ref):
    half = MINE // 2
    row = lax.broadcasted_iota(jnp.int32, (LANES, 2 * LANES), 0)
    channel = lax.broadcasted_iota(jnp.int32, (1, 2 * LANES), 1)
    place = jnp.where(row == channel // MINE * half + channel % half, 1.0, 0.0).astype(BF16)
    high = lax.broadcasted_iota(jnp.int32, (FRAMES, 2 * LANES), 1) // half % 2 == 1
    for n in range(CH // (2 * LANES)):
        owners = range(n * LANES // SHARE, (n + 1) * LANES // SHARE)
        rows = jnp.concatenate(
            [power_ref[pl.ds(PARTNERS.index(d) * SHARE, SHARE), :] for d in owners], axis=0
        )
        placed = lax.dot_general(
            rows, place, (((0,), (0,)), ((), ())), preferred_element_type=F32
        )
        out_ref[0, :, pl.ds(n * 2 * LANES, 2 * LANES)] = jnp.where(
            high, placed[FRAMES:], placed[:FRAMES]
        )


def order(power):
    return pl.pallas_call(
        order_kernel,
        name="order",
        out_shape=jax.ShapeDtypeStruct((1, FRAMES, CH), F32),
        compiler_params=pltpu.CompilerParams(vmem_limit_bytes=32 << 20),
    )(power)


def body(voltages, station_map, beam_table, weight_table, dm_trial):
    volts = voltages.reshape(STATIONS * FRAMES, NFFT)
    spectra = channelise(jnp.asarray(dft_table()), volts)
    signal = lax.all_to_all(
        spectra, "dom", split_axis=0, concat_axis=0, tiled=True, axis_index_groups=[PARTNERS]
    )
    weights, turns, choice = prep(station_map, beam_table, weight_table, dm_trial)
    power = form_beams(signal, weights, turns, choice, jnp.asarray(frame_table()))
    power = power.reshape(BEAMS, MINE // 2, LANES)
    power = lax.all_to_all(
        power,
        ("section", "dom"),
        split_axis=0,
        concat_axis=0,
        tiled=True,
        axis_index_groups=[EVERYONE],
    )
    return order(power.reshape(BEAMS * MINE // 2, LANES))


def solution(mesh):
    in_specs = (P("dom", None, None), P(), P(), P(None, None, "dom"), P())
    out_specs = P(("section", "dom"), None, None)
    return jax.shard_map(body, mesh=mesh, in_specs=in_specs, out_specs=out_specs, check_vma=False)
```

```python
import math

import jax
import jax.numpy as jnp
import ml_dtypes
import numpy as np
from jax import lax
from jax.experimental import pallas as pl
from jax.experimental.pallas import tpu as pltpu
from jax.sharding import PartitionSpec as P

NSTAT = 512
NFFT = 2048
CH = 1024
BEAMS = 128
NTAB = 64
FRAMES = 64
NDM = 32
SECTIONS = 4
DOMS = 32
STATIONS = NSTAT // DOMS
MINE = CH // (SECTIONS * DOMS)
LANES = 128
COLS = 2 * CH // SECTIONS
SHARE = SECTIONS * MINE // 2
STEPS = 4
STORES = 4
PIECE = NFFT // STEPS
NT = (((1,), (1,)), ((), ()))
GRID = (4, 4, 2)
PARTNERS = [int(d) for d in np.arange(DOMS).reshape(GRID).transpose(2, 1, 0).ravel()]
EVERYONE = [s * DOMS + d for d in PARTNERS for s in range(SECTIONS)]
F32 = jnp.float32
BF16 = jnp.bfloat16


def dft_table():
    sample = np.arange(NFFT)
    window = 0.5 - 0.5 * np.cos(sample.astype(np.float32) * np.float32(2.0 * math.pi / NFFT))
    scale = (window / np.float32(math.sqrt(NFFT))).astype(np.float32)
    angle = (np.arange(CH)[:, None] * sample[None, :] % NFFT).astype(np.float32) * np.float32(
        2.0 * math.pi / NFFT
    )
    parts = np.stack((np.cos(angle) * scale, -np.sin(angle) * scale))
    parts = parts.reshape(2, DOMS, SECTIONS, MINE, NFFT)[:, PARTNERS].transpose(2, 1, 0, 3, 4)
    return parts.reshape(SECTIONS, COLS, NFFT).astype(ml_dtypes.bfloat16)


def frame_table():
    index = np.arange(FRAMES)
    angle = (index[:, None] * index[None, :] % FRAMES) * (2.0 * math.pi / FRAMES)
    cosine, sine = np.cos(angle), np.sin(angle)
    table = np.block([[cosine, -sine], [sine, cosine]])
    high = table.astype(ml_dtypes.bfloat16)
    return np.stack((high, (table - high.astype(np.float64)).astype(ml_dtypes.bfloat16)))


def channelise_kernel(
    table_hbm, volts_hbm, out_hbm, table, volts, total, turned, out, table_sem, volts_sem, out_sem
):
    section = lax.axis_index("section")
    pieces = [pl.ds(n * PIECE, PIECE) for n in range(STEPS)]
    loads = [
        (
            pltpu.make_async_copy(table_hbm.at[section, :, p], table.at[:, p], table_sem.at[n]),
            pltpu.make_async_copy(volts_hbm.at[:, p], volts.at[:, p], volts_sem.at[n]),
        )
        for n, p in enumerate(pieces)
    ]
    for pair in loads:
        for load in pair:
            load.start()
    for n in range(STEPS - 1):
        for load in loads[n]:
            load.wait()
        term = lax.dot_general(
            table[:, pieces[n]], volts[:, pieces[n]], NT, preferred_element_type=F32
        )
        if n == 0:
            total[...] = term
        else:
            total[...] += term
    for load in loads[-1]:
        load.wait()
    low = lax.broadcasted_iota(jnp.int32, (8, LANES), 1) < FRAMES
    spectrum = total[...] + lax.dot_general(
        table[:, pieces[-1]], volts[:, pieces[-1]], NT, preferred_element_type=F32
    )
    for d in range(DOMS):
        for t in range(STATIONS // 2):
            real = spectrum[16 * d : 16 * d + 8, LANES * t : LANES * (t + 1)]
            imag = spectrum[16 * d + 8 : 16 * d + 16, LANES * t : LANES * (t + 1)]
            base = d * MINE * STATIONS + 2 * t
            turned[pl.ds(base, 8, stride=STATIONS), :] = jnp.where(
                low, real, pltpu.roll(imag, FRAMES, 1)
            )
            turned[pl.ds(base + 1, 8, stride=STATIONS), :] = jnp.where(
                low, pltpu.roll(real, FRAMES, 1), imag
            )
    stores = []
    for part in range(STORES):
        group = pl.ds(part * DOMS // STORES, DOMS // STORES)
        for d in range(part * DOMS // STORES, (part + 1) * DOMS // STORES):
            out[d] = turned[pl.ds(d * LANES, LANES), :].astype(BF16)
        stores.append(pltpu.make_async_copy(out.at[group], out_hbm.at[group], out_sem.at[part]))
        stores[-1].start()
    for store in stores:
        store.wait()


def channelise(table, volts):
    return pl.pallas_call(
        channelise_kernel,
        name="channelise",
        out_shape=jax.ShapeDtypeStruct((DOMS, MINE * STATIONS, LANES), BF16),
        in_specs=[pl.BlockSpec(memory_space=pl.ANY)] * 2,
        out_specs=pl.BlockSpec(memory_space=pl.ANY),
        scratch_shapes=[
            pltpu.VMEM((COLS, NFFT), BF16),
            pltpu.VMEM((STATIONS * FRAMES, NFFT), BF16),
            pltpu.VMEM((COLS, STATIONS * FRAMES), F32),
            pltpu.VMEM((DOMS * MINE * STATIONS, LANES), F32),
            pltpu.VMEM((DOMS, MINE * STATIONS, LANES), BF16),
            pltpu.SemaphoreType.DMA((STEPS,)),
            pltpu.SemaphoreType.DMA((STEPS,)),
            pltpu.SemaphoreType.DMA((STORES,)),
        ],
        compiler_params=pltpu.CompilerParams(vmem_limit_bytes=61 << 20),
        cost_estimate=pl.CostEstimate(
            flops=2 * COLS * NFFT * STATIONS * FRAMES, bytes_accessed=7 << 20, transcendentals=0
        ),
    )(table, volts)


def prep_kernel(map_ref, beam_ref, weight_ref, trial_ref, out_ref, turn_ref, choice_ref):
    section, dom = lax.axis_index("section"), lax.axis_index("dom")
    place = lax.broadcasted_iota(jnp.int32, (BEAMS, BEAMS), 0)
    beam = lax.broadcasted_iota(jnp.int32, (BEAMS, BEAMS), 1)
    z, y, x = place // 4 % 4, place // 16 % 4, place // 64
    owner = place % SECTIONS * DOMS + (z * 4 + y) * 2 + x
    swap = jnp.where(beam == owner, 1.0, 0.0).astype(BF16)
    station = lax.broadcasted_iota(jnp.int32, (NSTAT, NSTAT), 0)
    chosen = jnp.where(station == map_ref[...], 1.0, 0.0).astype(BF16)
    swapped = jnp.dot(swap, beam_ref[...].astype(F32).astype(BF16), preferred_element_type=F32)
    entries = jnp.dot(swapped.astype(BF16), chosen, preferred_element_type=F32).astype(jnp.int32)
    wanted = lax.broadcasted_iota(jnp.int32, (2 * NDM, BEAMS), 0) % NDM
    onehot = jnp.where(wanted == trial_ref[...], 1.0, 0.0).astype(BF16)
    choice_ref[...] = lax.dot_general(swap, onehot, NT, preferred_element_type=F32).astype(BF16)
    here = lax.broadcasted_iota(jnp.int32, (MINE, DOMS), 1)
    wanted = lax.broadcasted_iota(jnp.int32, (MINE, DOMS), 0) + section * MINE
    select = jnp.where(here == wanted, 1.0, 0.0).astype(BF16)
    weights = lax.dot_general(select, weight_ref[...], NT, preferred_element_type=F32)
    for j in range(MINE):
        row = jnp.broadcast_to(weights[j : j + 1, :], (BEAMS, LANES))
        for part in range(2):
            for t in range(NSTAT // LANES):
                which = entries[:, LANES * t : LANES * (t + 1)] + part * NTAB
                value = jnp.take_along_axis(row, which, axis=1)
                out_ref[j, pl.ds(part * BEAMS, BEAMS), pl.ds(LANES * t, LANES)] = value.astype(BF16)
    trial = lax.broadcasted_iota(jnp.int32, (NDM, LANES), 0)
    lane = lax.broadcasted_iota(jnp.int32, (NDM, LANES), 1)
    k = lane % FRAMES
    kappa = jnp.where(k < FRAMES // 2, k, k - FRAMES).astype(F32)
    measure = (trial + 1).astype(F32) / NDM
    for j in range(MINE):
        channel = jnp.full((NDM, LANES), dom * (SECTIONS * MINE) + section * MINE + j, jnp.int32)
        freq = 1.0 + channel.astype(F32) / CH
        spread = 1.0 / (freq * freq * freq)
        phase = math.pi * measure * spread * (kappa * kappa / FRAMES)
        sine = jnp.sin(phase)
        table = jnp.concatenate((jnp.cos(phase), jnp.where(lane < FRAMES, -sine, sine)), axis=1)
        top = table.astype(BF16)
        turn_ref[j, :NDM] = top
        turn_ref[j, NDM:] = (table - top.astype(F32)).astype(BF16)


def prep(station_map, beam_table, weight_table, dm_trial):
    return pl.pallas_call(
        prep_kernel,
        name="prep",
        out_shape=(
            jax.ShapeDtypeStruct((MINE, 2 * BEAMS, NSTAT), BF16),
            jax.ShapeDtypeStruct((MINE, 2 * NDM, 2 * LANES), BF16),
            jax.ShapeDtypeStruct((BEAMS, 2 * NDM), BF16),
        ),
        compiler_params=pltpu.CompilerParams(vmem_limit_bytes=32 << 20),
        cost_estimate=pl.CostEstimate(
            flops=4_000_000_000, bytes_accessed=16 << 20, transcendentals=65536
        ),
    )(
        station_map.reshape(*GRID, STATIONS).transpose(2, 1, 0, 3).reshape(1, NSTAT),
        beam_table,
        weight_table.reshape(2 * NTAB, weight_table.shape[2]),
        dm_trial.reshape(1, BEAMS),
    )


def split_dot(rows, high, low, turned):
    top = rows.astype(BF16)
    rest = (rows - top.astype(F32)).astype(BF16)
    side = int(turned)
    tables = jnp.concatenate(
        (
            jnp.concatenate((high, low), axis=1 - side),
            jnp.concatenate((high, jnp.zeros_like(high)), axis=1 - side),
        ),
        axis=side,
    )
    both = lax.dot_general(
        jnp.concatenate((top, rest), axis=1),
        tables,
        (((1,), (side,)), ((), ())),
        preferred_element_type=F32,
    )
    return both[:, :LANES] + both[:, LANES:]


def beam_kernel(signal_ref, weight_ref, turn_ref, choice_ref, frame_ref, out_ref, series, power):
    low = lax.broadcasted_iota(jnp.int32, (BEAMS, LANES), 1) < FRAMES
    for j in range(MINE):
        signal = signal_ref[:, pl.ds(j * STATIONS, STATIONS), :].reshape(NSTAT, LANES)
        product = jnp.dot(weight_ref[j], signal, preferred_element_type=F32)
        crossed = pltpu.roll(product[BEAMS:], FRAMES, 1)
        series[pl.ds(j * BEAMS, BEAMS), :] = product[:BEAMS] + jnp.where(low, -crossed, crossed)
    half = MINE // 2
    bins = split_dot(series[...], frame_ref[0], frame_ref[1], False)
    choice = choice_ref[...]
    turns = [jnp.dot(choice, turn_ref[j], preferred_element_type=F32) for j in range(MINE)]
    turn = jnp.concatenate(turns, axis=0)
    rotated = bins * turn[:, :LANES] + pltpu.roll(bins, FRAMES, 1) * turn[:, LANES:]
    result = split_dot(rotated, frame_ref[0], frame_ref[1], True) * (1.0 / FRAMES)
    square = result * result
    found = square + pltpu.roll(square, FRAMES, 1)
    for q in range(half):
        power[pl.ds(q, BEAMS, stride=half), :] = jnp.where(
            low,
            found[q * BEAMS : (q + 1) * BEAMS],
            found[(q + half) * BEAMS : (q + half + 1) * BEAMS],
        )
    out_ref[...] = power[...].astype(BF16)


def form_beams(signal, weights, turns, choice, frames):
    return pl.pallas_call(
        beam_kernel,
        name="beams",
        out_shape=jax.ShapeDtypeStruct((BEAMS * MINE // 2, LANES), BF16),
        scratch_shapes=[
            pltpu.VMEM((MINE * BEAMS, LANES), F32),
            pltpu.VMEM((BEAMS * MINE // 2, LANES), F32),
        ],
        compiler_params=pltpu.CompilerParams(vmem_limit_bytes=24 << 20),
        cost_estimate=pl.CostEstimate(
            flops=400_000_000, bytes_accessed=4 << 20, transcendentals=0
        ),
    )(signal, weights, turns, choice, frames)


def order_kernel(power_ref, out_hbm, out, sems):
    half = MINE // 2
    row = lax.broadcasted_iota(jnp.int32, (LANES, 2 * LANES), 0)
    channel = lax.broadcasted_iota(jnp.int32, (1, 2 * LANES), 1)
    place = jnp.where(row == channel // MINE * half + channel % half, 1.0, 0.0).astype(BF16)
    high = lax.broadcasted_iota(jnp.int32, (FRAMES, 2 * LANES), 1) // half % 2 == 1
    copies = []
    for n in range(CH // (2 * LANES)):
        owners = range(n * LANES // SHARE, (n + 1) * LANES // SHARE)
        rows = jnp.concatenate(
            [power_ref[pl.ds(PARTNERS.index(d) * SHARE, SHARE), :] for d in owners], axis=0
        )
        placed = lax.dot_general(
            rows, place, (((0,), (0,)), ((), ())), preferred_element_type=F32
        )
        block = pl.ds(n * 2 * LANES, 2 * LANES)
        out[0, :, block] = jnp.where(high, placed[FRAMES:], placed[:FRAMES])
        copies.append(
            pltpu.make_async_copy(out.at[:, :, block], out_hbm.at[:, :, block], sems.at[n])
        )
        copies[-1].start()
    for copy in copies:
        copy.wait()


def order(power):
    return pl.pallas_call(
        order_kernel,
        name="order",
        out_shape=jax.ShapeDtypeStruct((1, FRAMES, CH), F32),
        out_specs=pl.BlockSpec(memory_space=pl.ANY),
        scratch_shapes=[
            pltpu.VMEM((1, FRAMES, CH), F32),
            pltpu.SemaphoreType.DMA((CH // (2 * LANES),)),
        ],
        compiler_params=pltpu.CompilerParams(vmem_limit_bytes=32 << 20),
    )(power)


def body(voltages, station_map, beam_table, weight_table, dm_trial):
    volts = voltages.reshape(STATIONS * FRAMES, NFFT)
    spectra = channelise(jnp.asarray(dft_table()), volts)
    signal = lax.all_to_all(
        spectra, "dom", split_axis=0, concat_axis=0, tiled=True, axis_index_groups=[PARTNERS]
    )
    weights, turns, choice = prep(station_map, beam_table, weight_table, dm_trial)
    power = form_beams(signal, weights, turns, choice, jnp.asarray(frame_table()))
    power = power.reshape(BEAMS, MINE // 2, LANES)
    power = lax.all_to_all(
        power,
        ("section", "dom"),
        split_axis=0,
        concat_axis=0,
        tiled=True,
        axis_index_groups=[EVERYONE],
    )
    return order(power.reshape(BEAMS * MINE // 2, LANES))


def solution(mesh):
    in_specs = (P("dom", None, None), P(), P(), P(None, None, "dom"), P())
    out_specs = P(("section", "dom"), None, None)
    return jax.shard_map(body, mesh=mesh, in_specs=in_specs, out_specs=out_specs, check_vma=False)
```

```python
import math

import jax
import jax.numpy as jnp
import ml_dtypes
import numpy as np
from jax import lax
from jax.experimental import pallas as pl
from jax.experimental.pallas import tpu as pltpu
from jax.sharding import PartitionSpec as P

NSTAT = 512
NFFT = 2048
CH = 1024
BEAMS = 128
NTAB = 64
FRAMES = 64
NDM = 32
SECTIONS = 4
DOMS = 32
STATIONS = NSTAT // DOMS
MINE = CH // (SECTIONS * DOMS)
LANES = 128
COLS = 2 * CH // SECTIONS
SHARE = SECTIONS * MINE // 2
STEPS = 4
STORES = 4
PIECE = NFFT // STEPS
NT = (((1,), (1,)), ((), ()))
TN = (((0,), (0,)), ((), ()))
PARTNERS = [
    19, 31, 24, 9, 12, 2, 28, 8, 15, 17, 18, 26, 29, 6, 22, 20,
    14, 10, 3, 25, 11, 4, 21, 27, 30, 7, 5, 1, 23, 16, 0, 13,
]
EVERYONE = [s * DOMS + d for d in PARTNERS for s in range(SECTIONS)]
F32 = jnp.float32
BF16 = jnp.bfloat16


def dft_table():
    sample = np.arange(NFFT)
    window = 0.5 - 0.5 * np.cos(sample.astype(np.float32) * np.float32(2.0 * math.pi / NFFT))
    scale = (window / np.float32(math.sqrt(NFFT))).astype(np.float32)
    angle = (np.arange(CH)[:, None] * sample[None, :] % NFFT).astype(np.float32) * np.float32(
        2.0 * math.pi / NFFT
    )
    parts = np.stack((np.cos(angle) * scale, -np.sin(angle) * scale))
    parts = parts.reshape(2, DOMS, SECTIONS, MINE, NFFT)[:, PARTNERS].transpose(2, 1, 0, 3, 4)
    return parts.reshape(SECTIONS, COLS, NFFT).astype(ml_dtypes.bfloat16)


def frame_table():
    index = np.arange(FRAMES)
    angle = (index[:, None] * index[None, :] % FRAMES) * (2.0 * math.pi / FRAMES)
    cosine, sine = np.cos(angle), np.sin(angle)
    table = np.block([[cosine, -sine], [sine, cosine]])
    high = table.astype(ml_dtypes.bfloat16)
    return np.stack((high, (table - high.astype(np.float64)).astype(ml_dtypes.bfloat16)))


def channelise_kernel(
    table_hbm, volts_hbm, out_hbm, table, volts, total, turned, out, table_sem, volts_sem, out_sem
):
    section = lax.axis_index("section")
    pieces = [pl.ds(n * PIECE, PIECE) for n in range(STEPS)]
    loads = [
        (
            pltpu.make_async_copy(table_hbm.at[section, :, p], table.at[:, p], table_sem.at[n]),
            pltpu.make_async_copy(volts_hbm.at[:, p], volts.at[:, p], volts_sem.at[n]),
        )
        for n, p in enumerate(pieces)
    ]
    for pair in loads:
        for load in pair:
            load.start()
    for n in range(STEPS - 1):
        for load in loads[n]:
            load.wait()
        term = lax.dot_general(
            table[:, pieces[n]], volts[:, pieces[n]], NT, preferred_element_type=F32
        )
        if n == 0:
            total[...] = term
        else:
            total[...] += term
    for load in loads[-1]:
        load.wait()
    low = lax.broadcasted_iota(jnp.int32, (8, LANES), 1) < FRAMES
    spectrum = total[...] + lax.dot_general(
        table[:, pieces[-1]], volts[:, pieces[-1]], NT, preferred_element_type=F32
    )
    for d in range(DOMS):
        for t in range(STATIONS // 2):
            real = spectrum[16 * d : 16 * d + 8, LANES * t : LANES * (t + 1)]
            imag = spectrum[16 * d + 8 : 16 * d + 16, LANES * t : LANES * (t + 1)]
            base = d * MINE * STATIONS + 2 * t
            turned[pl.ds(base, 8, stride=STATIONS), :] = jnp.where(
                low, real, pltpu.roll(imag, FRAMES, 1)
            )
            turned[pl.ds(base + 1, 8, stride=STATIONS), :] = jnp.where(
                low, pltpu.roll(real, FRAMES, 1), imag
            )
    stores = []
    for part in range(STORES):
        group = pl.ds(part * DOMS // STORES, DOMS // STORES)
        for d in range(part * DOMS // STORES, (part + 1) * DOMS // STORES):
            out[d] = turned[pl.ds(d * LANES, LANES), :].astype(BF16)
        stores.append(pltpu.make_async_copy(out.at[group], out_hbm.at[group], out_sem.at[part]))
        stores[-1].start()
    for store in stores:
        store.wait()


def channelise(table, volts):
    return pl.pallas_call(
        channelise_kernel,
        name="channelise",
        out_shape=jax.ShapeDtypeStruct((DOMS, MINE * STATIONS, LANES), BF16),
        in_specs=[pl.BlockSpec(memory_space=pl.ANY)] * 2,
        out_specs=pl.BlockSpec(memory_space=pl.ANY),
        scratch_shapes=[
            pltpu.VMEM((COLS, NFFT), BF16),
            pltpu.VMEM((STATIONS * FRAMES, NFFT), BF16),
            pltpu.VMEM((COLS, STATIONS * FRAMES), F32),
            pltpu.VMEM((DOMS * MINE * STATIONS, LANES), F32),
            pltpu.VMEM((DOMS, MINE * STATIONS, LANES), BF16),
            pltpu.SemaphoreType.DMA((STEPS,)),
            pltpu.SemaphoreType.DMA((STEPS,)),
            pltpu.SemaphoreType.DMA((STORES,)),
        ],
        compiler_params=pltpu.CompilerParams(vmem_limit_bytes=61 << 20),
        cost_estimate=pl.CostEstimate(
            flops=2 * COLS * NFFT * STATIONS * FRAMES, bytes_accessed=7 << 20, transcendentals=0
        ),
    )(table, volts)


def prep_kernel(map_ref, owner_ref, beam_ref, weight_ref, trial_ref, out_ref, turn_ref, choice_ref):
    section, dom = lax.axis_index("section"), lax.axis_index("dom")
    beam = lax.broadcasted_iota(jnp.int32, (BEAMS, BEAMS), 0)
    swap = jnp.where(beam == owner_ref[...], 1.0, 0.0).astype(BF16)
    station = lax.broadcasted_iota(jnp.int32, (NSTAT, NSTAT), 0)
    chosen = jnp.where(station == map_ref[...], 1.0, 0.0).astype(BF16)
    table = beam_ref[...].astype(F32).astype(BF16)
    swapped = lax.dot_general(swap, table, TN, preferred_element_type=F32)
    entries = jnp.dot(swapped.astype(BF16), chosen, preferred_element_type=F32).astype(jnp.int32)
    wanted = lax.broadcasted_iota(jnp.int32, (2 * NDM, BEAMS), 0) % NDM
    onehot = jnp.where(wanted == trial_ref[...], 1.0, 0.0).astype(BF16)
    choice = lax.dot_general(swap, onehot, (((0,), (1,)), ((), ())), preferred_element_type=F32)
    choice_ref[...] = choice.astype(BF16)
    here = lax.broadcasted_iota(jnp.int32, (MINE, DOMS), 1)
    wanted = lax.broadcasted_iota(jnp.int32, (MINE, DOMS), 0) + section * MINE
    select = jnp.where(here == wanted, 1.0, 0.0).astype(BF16)
    weights = lax.dot_general(select, weight_ref[...], NT, preferred_element_type=F32)
    for j in range(MINE):
        row = jnp.broadcast_to(weights[j : j + 1, :], (BEAMS, LANES))
        for part in range(2):
            for t in range(NSTAT // LANES):
                which = entries[:, LANES * t : LANES * (t + 1)] + part * NTAB
                value = jnp.take_along_axis(row, which, axis=1)
                out_ref[j, pl.ds(part * BEAMS, BEAMS), pl.ds(LANES * t, LANES)] = value.astype(BF16)
    trial = lax.broadcasted_iota(jnp.int32, (NDM, LANES), 0)
    lane = lax.broadcasted_iota(jnp.int32, (NDM, LANES), 1)
    k = lane % FRAMES
    kappa = jnp.where(k < FRAMES // 2, k, k - FRAMES).astype(F32)
    measure = (trial + 1).astype(F32) / NDM
    for j in range(MINE):
        channel = jnp.full((NDM, LANES), dom * (SECTIONS * MINE) + section * MINE + j, jnp.int32)
        freq = 1.0 + channel.astype(F32) / CH
        spread = 1.0 / (freq * freq * freq)
        phase = math.pi * measure * spread * (kappa * kappa / FRAMES)
        sine = jnp.sin(phase)
        table = jnp.concatenate((jnp.cos(phase), jnp.where(lane < FRAMES, -sine, sine)), axis=1)
        top = table.astype(BF16)
        turn_ref[j, :NDM] = top
        turn_ref[j, NDM:] = (table - top.astype(F32)).astype(BF16)


def prep(station_map, beam_table, weight_table, dm_trial):
    rows = station_map.reshape(DOMS, STATIONS)
    return pl.pallas_call(
        prep_kernel,
        name="prep",
        out_shape=(
            jax.ShapeDtypeStruct((MINE, 2 * BEAMS, NSTAT), BF16),
            jax.ShapeDtypeStruct((MINE, 2 * NDM, 2 * LANES), BF16),
            jax.ShapeDtypeStruct((BEAMS, 2 * NDM), BF16),
        ),
        compiler_params=pltpu.CompilerParams(vmem_limit_bytes=32 << 20),
        cost_estimate=pl.CostEstimate(
            flops=4_000_000_000, bytes_accessed=16 << 20, transcendentals=65536
        ),
    )(
        jnp.concatenate([rows[d] for d in PARTNERS]).reshape(1, NSTAT),
        jnp.asarray(np.array(EVERYONE, np.int32).reshape(1, BEAMS)),
        beam_table,
        weight_table.reshape(2 * NTAB, weight_table.shape[2]),
        dm_trial.reshape(1, BEAMS),
    )


def split_dot(rows, high, low, turned):
    top = rows.astype(BF16)
    rest = (rows - top.astype(F32)).astype(BF16)
    side = int(turned)
    tables = jnp.concatenate(
        (
            jnp.concatenate((high, low), axis=1 - side),
            jnp.concatenate((high, jnp.zeros_like(high)), axis=1 - side),
        ),
        axis=side,
    )
    both = lax.dot_general(
        jnp.concatenate((top, rest), axis=1),
        tables,
        (((1,), (side,)), ((), ())),
        preferred_element_type=F32,
    )
    return both[:, :LANES] + both[:, LANES:]


def beam_kernel(signal_ref, weight_ref, turn_ref, choice_ref, frame_ref, out_ref, series, power):
    low = lax.broadcasted_iota(jnp.int32, (BEAMS, LANES), 1) < FRAMES
    for j in range(MINE):
        signal = signal_ref[:, pl.ds(j * STATIONS, STATIONS), :].reshape(NSTAT, LANES)
        product = jnp.dot(weight_ref[j], signal, preferred_element_type=F32)
        crossed = pltpu.roll(product[BEAMS:], FRAMES, 1)
        series[pl.ds(j * BEAMS, BEAMS), :] = product[:BEAMS] + jnp.where(low, -crossed, crossed)
    half = MINE // 2
    bins = split_dot(series[...], frame_ref[0], frame_ref[1], False)
    choice = choice_ref[...]
    turns = [jnp.dot(choice, turn_ref[j], preferred_element_type=F32) for j in range(MINE)]
    turn = jnp.concatenate(turns, axis=0)
    rotated = bins * turn[:, :LANES] + pltpu.roll(bins, FRAMES, 1) * turn[:, LANES:]
    result = split_dot(rotated, frame_ref[0], frame_ref[1], True) * (1.0 / FRAMES)
    square = result * result
    found = square + pltpu.roll(square, FRAMES, 1)
    for q in range(half):
        power[pl.ds(q, BEAMS, stride=half), :] = jnp.where(
            low,
            found[q * BEAMS : (q + 1) * BEAMS],
            found[(q + half) * BEAMS : (q + half + 1) * BEAMS],
        )
    out_ref[...] = power[...].astype(BF16)


def form_beams(signal, weights, turns, choice, frames):
    return pl.pallas_call(
        beam_kernel,
        name="beams",
        out_shape=jax.ShapeDtypeStruct((BEAMS * MINE // 2, LANES), BF16),
        scratch_shapes=[
            pltpu.VMEM((MINE * BEAMS, LANES), F32),
            pltpu.VMEM((BEAMS * MINE // 2, LANES), F32),
        ],
        compiler_params=pltpu.CompilerParams(vmem_limit_bytes=24 << 20),
        cost_estimate=pl.CostEstimate(
            flops=400_000_000, bytes_accessed=4 << 20, transcendentals=0
        ),
    )(signal, weights, turns, choice, frames)


def order_kernel(power_ref, out_hbm, out, sems):
    half = MINE // 2
    row = lax.broadcasted_iota(jnp.int32, (LANES, 2 * LANES), 0)
    channel = lax.broadcasted_iota(jnp.int32, (1, 2 * LANES), 1)
    place = jnp.where(row == channel // MINE * half + channel % half, 1.0, 0.0).astype(BF16)
    high = lax.broadcasted_iota(jnp.int32, (FRAMES, 2 * LANES), 1) // half % 2 == 1
    copies = []
    for n in range(CH // (2 * LANES)):
        owners = range(n * LANES // SHARE, (n + 1) * LANES // SHARE)
        rows = jnp.concatenate(
            [power_ref[pl.ds(PARTNERS.index(d) * SHARE, SHARE), :] for d in owners], axis=0
        )
        placed = lax.dot_general(
            rows, place, TN, preferred_element_type=F32
        )
        block = pl.ds(n * 2 * LANES, 2 * LANES)
        out[0, :, block] = jnp.where(high, placed[FRAMES:], placed[:FRAMES])
        copies.append(
            pltpu.make_async_copy(out.at[:, :, block], out_hbm.at[:, :, block], sems.at[n])
        )
        copies[-1].start()
    for copy in copies:
        copy.wait()


def order(power):
    return pl.pallas_call(
        order_kernel,
        name="order",
        out_shape=jax.ShapeDtypeStruct((1, FRAMES, CH), F32),
        out_specs=pl.BlockSpec(memory_space=pl.ANY),
        scratch_shapes=[
            pltpu.VMEM((1, FRAMES, CH), F32),
            pltpu.SemaphoreType.DMA((CH // (2 * LANES),)),
        ],
        compiler_params=pltpu.CompilerParams(vmem_limit_bytes=32 << 20),
    )(power)


def body(voltages, station_map, beam_table, weight_table, dm_trial):
    volts = voltages.reshape(STATIONS * FRAMES, NFFT)
    spectra = channelise(jnp.asarray(dft_table()), volts)
    signal = lax.all_to_all(
        spectra, "dom", split_axis=0, concat_axis=0, tiled=True, axis_index_groups=[PARTNERS]
    )
    weights, turns, choice = prep(station_map, beam_table, weight_table, dm_trial)
    power = form_beams(signal, weights, turns, choice, jnp.asarray(frame_table()))
    power = power.reshape(BEAMS, MINE // 2, LANES)
    power = lax.all_to_all(
        power,
        ("section", "dom"),
        split_axis=0,
        concat_axis=0,
        tiled=True,
        axis_index_groups=[EVERYONE],
    )
    return order(power.reshape(BEAMS * MINE // 2, LANES))


def solution(mesh):
    in_specs = (P("dom", None, None), P(), P(), P(None, None, "dom"), P())
    out_specs = P(("section", "dom"), None, None)
    return jax.shard_map(body, mesh=mesh, in_specs=in_specs, out_specs=out_specs, check_vma=False)
```

```python
import math

import jax
import jax.numpy as jnp
import ml_dtypes
import numpy as np
from jax import lax
from jax.experimental import pallas as pl
from jax.experimental.pallas import tpu as pltpu
from jax.sharding import PartitionSpec as P

NSTAT = 512
NFFT = 2048
CH = 1024
BEAMS = 128
NTAB = 64
FRAMES = 64
NDM = 32
SECTIONS = 4
DOMS = 32
STATIONS = NSTAT // DOMS
MINE = CH // (SECTIONS * DOMS)
LANES = 128
COLS = 2 * CH // SECTIONS
SHARE = SECTIONS * MINE // 2
STEPS = 4
STORES = 8
PIECE = NFFT // STEPS
NT = (((1,), (1,)), ((), ()))
TN = (((0,), (0,)), ((), ()))
PARTNERS = [
    27, 2, 11, 21, 0, 3, 14, 9, 6, 13, 1, 12, 23, 4, 29, 25,
    18, 31, 22, 19, 24, 5, 16, 17, 30, 15, 8, 28, 26, 7, 20, 10,
]
EVERYONE = [s * DOMS + d for d in PARTNERS for s in range(SECTIONS)]
F32 = jnp.float32
BF16 = jnp.bfloat16


def dft_table():
    sample = np.arange(NFFT)
    window = 0.5 - 0.5 * np.cos(sample.astype(np.float32) * np.float32(2.0 * math.pi / NFFT))
    scale = (window / np.float32(math.sqrt(NFFT))).astype(np.float32)
    angle = (np.arange(CH)[:, None] * sample[None, :] % NFFT).astype(np.float32) * np.float32(
        2.0 * math.pi / NFFT
    )
    parts = np.stack((np.cos(angle) * scale, -np.sin(angle) * scale))
    parts = parts.reshape(2, DOMS, SECTIONS, MINE, NFFT)[:, PARTNERS].transpose(2, 1, 0, 3, 4)
    return parts.reshape(SECTIONS, COLS, NFFT).astype(ml_dtypes.bfloat16)


def frame_table():
    index = np.arange(FRAMES)
    angle = (index[:, None] * index[None, :] % FRAMES) * (2.0 * math.pi / FRAMES)
    cosine, sine = np.cos(angle), np.sin(angle)
    table = np.block([[cosine, -sine], [sine, cosine]])
    high = table.astype(ml_dtypes.bfloat16)
    return np.stack((high, (table - high.astype(np.float64)).astype(ml_dtypes.bfloat16)))


def channelise_kernel(
    table_hbm, volts_hbm, out_hbm, table, volts, total, turned, out, table_sem, volts_sem, out_sem
):
    section = lax.axis_index("section")
    pieces = [pl.ds(n * PIECE, PIECE) for n in range(STEPS)]
    loads = [
        (
            pltpu.make_async_copy(table_hbm.at[section, :, p], table.at[:, p], table_sem.at[n]),
            pltpu.make_async_copy(volts_hbm.at[:, p], volts.at[:, p], volts_sem.at[n]),
        )
        for n, p in enumerate(pieces)
    ]
    for pair in loads:
        for load in pair:
            load.start()
    for n in range(STEPS - 1):
        for load in loads[n]:
            load.wait()
        term = lax.dot_general(
            table[:, pieces[n]], volts[:, pieces[n]], NT, preferred_element_type=F32
        )
        if n == 0:
            total[...] = term
        else:
            total[...] += term
    for load in loads[-1]:
        load.wait()
    low = lax.broadcasted_iota(jnp.int32, (8, LANES), 1) < FRAMES
    spectrum = total[...] + lax.dot_general(
        table[:, pieces[-1]], volts[:, pieces[-1]], NT, preferred_element_type=F32
    )
    for d in range(DOMS):
        for t in range(STATIONS // 2):
            real = spectrum[16 * d : 16 * d + 8, LANES * t : LANES * (t + 1)]
            imag = spectrum[16 * d + 8 : 16 * d + 16, LANES * t : LANES * (t + 1)]
            base = d * MINE * STATIONS + 2 * t
            turned[pl.ds(base, 8, stride=STATIONS), :] = jnp.where(
                low, real, pltpu.roll(imag, FRAMES, 1)
            )
            turned[pl.ds(base + 1, 8, stride=STATIONS), :] = jnp.where(
                low, pltpu.roll(real, FRAMES, 1), imag
            )
    stores = []
    for part in range(STORES):
        group = pl.ds(part * DOMS // STORES, DOMS // STORES)
        for d in range(part * DOMS // STORES, (part + 1) * DOMS // STORES):
            out[d] = turned[pl.ds(d * LANES, LANES), :].astype(BF16)
        stores.append(pltpu.make_async_copy(out.at[group], out_hbm.at[group], out_sem.at[part]))
        stores[-1].start()
    for store in stores:
        store.wait()


def channelise(table, volts):
    return pl.pallas_call(
        channelise_kernel,
        name="channelise",
        out_shape=jax.ShapeDtypeStruct((DOMS, MINE * STATIONS, LANES), BF16),
        in_specs=[pl.BlockSpec(memory_space=pl.ANY)] * 2,
        out_specs=pl.BlockSpec(memory_space=pl.ANY),
        scratch_shapes=[
            pltpu.VMEM((COLS, NFFT), BF16),
            pltpu.VMEM((STATIONS * FRAMES, NFFT), BF16),
            pltpu.VMEM((COLS, STATIONS * FRAMES), F32),
            pltpu.VMEM((DOMS * MINE * STATIONS, LANES), F32),
            pltpu.VMEM((DOMS, MINE * STATIONS, LANES), BF16),
            pltpu.SemaphoreType.DMA((STEPS,)),
            pltpu.SemaphoreType.DMA((STEPS,)),
            pltpu.SemaphoreType.DMA((STORES,)),
        ],
        compiler_params=pltpu.CompilerParams(vmem_limit_bytes=61 << 20),
        cost_estimate=pl.CostEstimate(
            flops=2 * COLS * NFFT * STATIONS * FRAMES, bytes_accessed=7 << 20, transcendentals=0
        ),
    )(table, volts)


def prep_kernel(map_ref, owner_ref, beam_ref, weight_ref, trial_ref, out_ref, turn_ref, choice_ref):
    section, dom = lax.axis_index("section"), lax.axis_index("dom")
    beam = lax.broadcasted_iota(jnp.int32, (BEAMS, BEAMS), 0)
    swap = jnp.where(beam == owner_ref[...], 1.0, 0.0).astype(BF16)
    station = lax.broadcasted_iota(jnp.int32, (NSTAT, NSTAT), 0)
    chosen = jnp.where(station == map_ref[...], 1.0, 0.0).astype(BF16)
    table = beam_ref[...].astype(F32).astype(BF16)
    swapped = lax.dot_general(swap, table, TN, preferred_element_type=F32)
    entries = jnp.dot(swapped.astype(BF16), chosen, preferred_element_type=F32).astype(jnp.int32)
    wanted = lax.broadcasted_iota(jnp.int32, (2 * NDM, BEAMS), 0) % NDM
    onehot = jnp.where(wanted == trial_ref[...], 1.0, 0.0).astype(BF16)
    choice = lax.dot_general(swap, onehot, (((0,), (1,)), ((), ())), preferred_element_type=F32)
    choice_ref[...] = choice.astype(BF16)
    here = lax.broadcasted_iota(jnp.int32, (MINE, DOMS), 1)
    wanted = lax.broadcasted_iota(jnp.int32, (MINE, DOMS), 0) + section * MINE
    select = jnp.where(here == wanted, 1.0, 0.0).astype(BF16)
    weights = lax.dot_general(select, weight_ref[...], NT, preferred_element_type=F32)
    for j in range(MINE):
        row = jnp.broadcast_to(weights[j : j + 1, :], (BEAMS, LANES))
        for part in range(2):
            for t in range(NSTAT // LANES):
                which = entries[:, LANES * t : LANES * (t + 1)] + part * NTAB
                value = jnp.take_along_axis(row, which, axis=1)
                out_ref[j, pl.ds(part * BEAMS, BEAMS), pl.ds(LANES * t, LANES)] = value.astype(BF16)
    trial = lax.broadcasted_iota(jnp.int32, (NDM, LANES), 0)
    lane = lax.broadcasted_iota(jnp.int32, (NDM, LANES), 1)
    k = lane % FRAMES
    kappa = jnp.where(k < FRAMES // 2, k, k - FRAMES).astype(F32)
    measure = (trial + 1).astype(F32) / NDM
    for j in range(MINE):
        channel = jnp.full((NDM, LANES), dom * (SECTIONS * MINE) + section * MINE + j, jnp.int32)
        freq = 1.0 + channel.astype(F32) / CH
        spread = 1.0 / (freq * freq * freq)
        phase = math.pi * measure * spread * (kappa * kappa / FRAMES)
        sine = jnp.sin(phase)
        table = jnp.concatenate((jnp.cos(phase), jnp.where(lane < FRAMES, -sine, sine)), axis=1)
        top = table.astype(BF16)
        turn_ref[j, :NDM] = top
        turn_ref[j, NDM:] = (table - top.astype(F32)).astype(BF16)


def prep(station_map, beam_table, weight_table, dm_trial):
    rows = station_map.reshape(DOMS, STATIONS)
    return pl.pallas_call(
        prep_kernel,
        name="prep",
        out_shape=(
            jax.ShapeDtypeStruct((MINE, 2 * BEAMS, NSTAT), BF16),
            jax.ShapeDtypeStruct((MINE, 2 * NDM, 2 * LANES), BF16),
            jax.ShapeDtypeStruct((BEAMS, 2 * NDM), BF16),
        ),
        compiler_params=pltpu.CompilerParams(vmem_limit_bytes=32 << 20),
        cost_estimate=pl.CostEstimate(
            flops=4_000_000_000, bytes_accessed=16 << 20, transcendentals=65536
        ),
    )(
        jnp.concatenate([rows[d] for d in PARTNERS]).reshape(1, NSTAT),
        jnp.asarray(np.array(EVERYONE, np.int32).reshape(1, BEAMS)),
        beam_table,
        weight_table.reshape(2 * NTAB, weight_table.shape[2]),
        dm_trial.reshape(1, BEAMS),
    )


def split_dot(rows, high, low, turned):
    top = rows.astype(BF16)
    rest = (rows - top.astype(F32)).astype(BF16)
    side = int(turned)
    tables = jnp.concatenate(
        (
            jnp.concatenate((high, low), axis=1 - side),
            jnp.concatenate((high, jnp.zeros_like(high)), axis=1 - side),
        ),
        axis=side,
    )
    both = lax.dot_general(
        jnp.concatenate((top, rest), axis=1),
        tables,
        (((1,), (side,)), ((), ())),
        preferred_element_type=F32,
    )
    return both[:, :LANES] + both[:, LANES:]


def beam_kernel(signal_ref, weight_ref, turn_ref, choice_ref, frame_ref, out_ref, series, power):
    low = lax.broadcasted_iota(jnp.int32, (BEAMS, LANES), 1) < FRAMES
    for j in range(MINE):
        signal = signal_ref[:, pl.ds(j * STATIONS, STATIONS), :].reshape(NSTAT, LANES)
        product = jnp.dot(weight_ref[j], signal, preferred_element_type=F32)
        crossed = pltpu.roll(product[BEAMS:], FRAMES, 1)
        series[pl.ds(j * BEAMS, BEAMS), :] = product[:BEAMS] + jnp.where(low, -crossed, crossed)
    half = MINE // 2
    bins = split_dot(series[...], frame_ref[0], frame_ref[1], False)
    choice = choice_ref[...]
    turns = [jnp.dot(choice, turn_ref[j], preferred_element_type=F32) for j in range(MINE)]
    turn = jnp.concatenate(turns, axis=0)
    rotated = bins * turn[:, :LANES] + pltpu.roll(bins, FRAMES, 1) * turn[:, LANES:]
    result = split_dot(rotated, frame_ref[0], frame_ref[1], True) * (1.0 / FRAMES)
    square = result * result
    found = square + pltpu.roll(square, FRAMES, 1)
    for q in range(half):
        power[pl.ds(q, BEAMS, stride=half), :] = jnp.where(
            low,
            found[q * BEAMS : (q + 1) * BEAMS],
            found[(q + half) * BEAMS : (q + half + 1) * BEAMS],
        )
    out_ref[...] = power[...].astype(BF16)


def form_beams(signal, weights, turns, choice, frames):
    return pl.pallas_call(
        beam_kernel,
        name="beams",
        out_shape=jax.ShapeDtypeStruct((BEAMS * MINE // 2, LANES), BF16),
        scratch_shapes=[
            pltpu.VMEM((MINE * BEAMS, LANES), F32),
            pltpu.VMEM((BEAMS * MINE // 2, LANES), F32),
        ],
        compiler_params=pltpu.CompilerParams(vmem_limit_bytes=24 << 20),
        cost_estimate=pl.CostEstimate(
            flops=400_000_000, bytes_accessed=4 << 20, transcendentals=0
        ),
    )(signal, weights, turns, choice, frames)


def order_kernel(power_ref, out_hbm, out, sems):
    half = MINE // 2
    row = lax.broadcasted_iota(jnp.int32, (LANES, 2 * LANES), 0)
    channel = lax.broadcasted_iota(jnp.int32, (1, 2 * LANES), 1)
    place = jnp.where(row == channel // MINE * half + channel % half, 1.0, 0.0).astype(BF16)
    high = lax.broadcasted_iota(jnp.int32, (FRAMES, 2 * LANES), 1) // half % 2 == 1
    copies = []
    for n in range(CH // (2 * LANES)):
        owners = range(n * LANES // SHARE, (n + 1) * LANES // SHARE)
        rows = jnp.concatenate(
            [power_ref[pl.ds(PARTNERS.index(d) * SHARE, SHARE), :] for d in owners], axis=0
        )
        placed = lax.dot_general(
            rows, place, TN, preferred_element_type=F32
        )
        block = pl.ds(n * 2 * LANES, 2 * LANES)
        out[0, :, block] = jnp.where(high, placed[FRAMES:], placed[:FRAMES])
        copies.append(
            pltpu.make_async_copy(out.at[:, :, block], out_hbm.at[:, :, block], sems.at[n])
        )
        copies[-1].start()
    for copy in copies:
        copy.wait()


def order(power):
    return pl.pallas_call(
        order_kernel,
        name="order",
        out_shape=jax.ShapeDtypeStruct((1, FRAMES, CH), F32),
        out_specs=pl.BlockSpec(memory_space=pl.ANY),
        scratch_shapes=[
            pltpu.VMEM((1, FRAMES, CH), F32),
            pltpu.SemaphoreType.DMA((CH // (2 * LANES),)),
        ],
        compiler_params=pltpu.CompilerParams(vmem_limit_bytes=32 << 20),
    )(power)


def body(voltages, station_map, beam_table, weight_table, dm_trial):
    volts = voltages.reshape(STATIONS * FRAMES, NFFT)
    spectra = channelise(jnp.asarray(dft_table()), volts)
    signal = lax.all_to_all(
        spectra, "dom", split_axis=0, concat_axis=0, tiled=True, axis_index_groups=[PARTNERS]
    )
    weights, turns, choice = prep(station_map, beam_table, weight_table, dm_trial)
    power = form_beams(signal, weights, turns, choice, jnp.asarray(frame_table()))
    power = power.reshape(BEAMS, MINE // 2, LANES)
    power = lax.all_to_all(
        power,
        ("section", "dom"),
        split_axis=0,
        concat_axis=0,
        tiled=True,
        axis_index_groups=[EVERYONE],
    )
    return order(power.reshape(BEAMS * MINE // 2, LANES))


def solution(mesh):
    in_specs = (P("dom", None, None), P(), P(), P(None, None, "dom"), P())
    out_specs = P(("section", "dom"), None, None)
    return jax.shard_map(body, mesh=mesh, in_specs=in_specs, out_specs=out_specs, check_vma=False)
```
